32 devices in a mesh: section: 8 (over y, x, core), head: 4 (over z).
Axes of the slice: x: 2, y: 2, z: 4, core: 2. Of those that a mesh axis runs over, the one named last changes fastest.
Arguments:
- residual: bfloat16 [2048, 2, 4096], P(('section', 'head')), may hold values from -3 to 3
- queries: bfloat16 [2, 2048, 4096], P(None, 'section', 'head'), may hold values from -80 to 80
- new_kv: bfloat16 [2, 2, 2048, 1024], P(None, None, 'section'), may hold values from -6 to 6
- cache_kv: bfloat16 [2, 12288, 1024], P(None, 'section'), may hold values from -6 to 6
- lengths: int32 [8], replicated, may hold values from 1 to 1536, as said below
- out_weight: bfloat16 [8, 4096, 4096], P('section', 'head'), may hold values from -0.09375 to 0.09375
Outputs:
- advanced: bfloat16 [2048, 2, 4096], P(('section', 'head'))
The draws below stay inside these ranges and needn't reach their ends.
Inputs may be any that keep to these rules, and one draw needn't show every extreme that they name: `lengths`: some section's cache holds 1536 positions while the section half the sections away holds at most 128.
All inputs are finite; a program needn't handle non-finite values.
Results may differ from the reference program's by a relative error of at most 0.013.
Values may be sent and summed in bfloat16 or wider, within the bound.
No kernel may reach another device: no remote copies, remote signals or barrier semaphores. Data moves between devices by JAX's collectives and lax.ppermute only.
A program may use at most 64 MiB of HBM per device.

```python
import math
import jax
import jax.numpy as jnp
from jax import lax

D = 4096
QH = 32
KVH = 8
HD = 128
ROWS = 256
BLK = 128
TICKS = 2
SECTIONS = 8
TOKENS = 2048
CMAX = 1536
N_HEAD = 4


def draw_queries(key, part):
    first_key = jax.random.fold_in(key, 11)
    shape_now = (TICKS, SECTIONS, ROWS, QH * HD)
    values = jnp.clip(jax.random.normal(first_key, shape_now, jnp.float32), -5.0, 5.0)
    return values.reshape(TICKS, TOKENS, QH * HD).astype(jnp.bfloat16)


def draw_new_kv(key, part):
    first_key = jax.random.fold_in(key, 21)
    shape_now = (TICKS, 2, SECTIONS, ROWS, KVH * HD)
    values = jnp.clip(jax.random.normal(first_key, shape_now, jnp.float32), -5.0, 5.0)
    return values.reshape(TICKS, 2, TOKENS, KVH * HD).astype(jnp.bfloat16)


def draw_cache_kv(key, part):
    first_key = jax.random.fold_in(key, 31)
    shape_now = (2, SECTIONS, CMAX, KVH * HD)
    values = jnp.clip(jax.random.normal(first_key, shape_now, jnp.float32), -5.0, 5.0)
    return values.reshape(2, SECTIONS * CMAX, KVH * HD).astype(jnp.bfloat16)


def draw_lengths(key, part):
    first_draw = jax.random.randint(jax.random.fold_in(key, 41), (SECTIONS,), 1, CMAX + 1)
    second_draw = jax.random.randint(jax.random.fold_in(key, 42), (SECTIONS,), 1, CMAX + 1)
    lengths = jnp.minimum(first_draw, second_draw).astype(jnp.int32)
    chosen = jax.random.randint(jax.random.fold_in(key, 43), (), 0, SECTIONS // 2)
    short_length = jax.random.randint(jax.random.fold_in(key, 44), (), 1, BLK + 1)
    section_ids = jnp.arange(SECTIONS, dtype=jnp.int32)
    lengths = jnp.where(section_ids == chosen, CMAX, lengths)
    lengths = jnp.where(section_ids == chosen + SECTIONS // 2, short_length, lengths)
    return lengths.astype(jnp.int32)


def block_levels(stream_key, shape, shards, low, top_value):
    level = 1.0
    for position, blocks in shards:
        steps = jax.random.uniform(jax.random.fold_in(jax.random.fold_in(stream_key, 6), position), (blocks,), jnp.float32, low / len(shards), top_value / len(shards))
        level = level * jnp.repeat(jnp.exp(steps), shape[position] // blocks).reshape((-1,) + (1,) * (len(shape) - 1 - position))
    return level


def normal_values(key, dims, spread, reach, split=(), kind=jnp.bfloat16):
    entries = jax.random.normal(key, dims, jnp.float32) * spread
    if len(split) > 0:
        entries = block_levels(key, dims, split, -0.22, 0.18) * entries
    return jnp.clip(entries, min=-reach, max=reach).astype(kind)


def setup_inputs(seed: int = 0) -> dict:
    key_of = jax.random.split(jax.random.key(seed), 7)
    residual = normal_values(key_of[0], (TOKENS, TICKS, D), 0.5, 3.0, ((0, 32),))
    queries = draw_queries(jax.random.fold_in(key_of[6], 71), 0)
    new_kv = draw_new_kv(jax.random.fold_in(key_of[6], 71), 0)
    cache_kv = draw_cache_kv(jax.random.fold_in(key_of[6], 71), 0)
    lengths = draw_lengths(jax.random.fold_in(key_of[6], 71), 0)
    out_weight = normal_values(key_of[5], (SECTIONS, QH * HD, D), (QH * HD) ** -0.5, 0.09375, ((0, 8), (1, 4)))
    return dict(residual=residual, queries=queries, new_kv=new_kv, cache_kv=cache_kv, lengths=lengths, out_weight=out_weight)


def section_heads(query_now, fresh_now, cache_now, length_now):
    group_size = QH // KVH
    key_count = CMAX + TICKS * ROWS
    key_rows = jnp.concatenate([cache_now[0]] + [fresh_now[earlier, 0] for earlier in range(TICKS)], axis=0)
    value_rows = jnp.concatenate([cache_now[1]] + [fresh_now[earlier, 1] for earlier in range(TICKS)], axis=0)
    key_rows = key_rows.astype(jnp.float32).reshape(key_count, KVH, HD)
    value_rows = value_rows.astype(jnp.float32).reshape(key_count, KVH, HD)
    key_slot = jnp.arange(key_count)
    in_cache = key_slot < CMAX
    cache_used = key_slot < length_now
    fresh_tick = (key_slot - CMAX) // ROWS
    fresh_row = (key_slot - CMAX) % ROWS
    row_index = jnp.arange(ROWS)
    results = []
    for tick_now in range(TICKS):
        later = (fresh_tick[None, :] < tick_now) | (fresh_tick[None, :] == tick_now) & (fresh_row[None, :] <= row_index[:, None])
        visible = jnp.where(in_cache[None, :], cache_used[None, :], later)
        query_rows = query_now[tick_now].astype(jnp.float32).reshape(ROWS, KVH, group_size, HD)
        scores = jnp.einsum('rkgd,lkd->kgrl', query_rows, key_rows, precision=lax.Precision.HIGHEST) / math.sqrt(HD)
        scores = jnp.where(visible[None, None], scores, -1e+30)
        highest = lax.optimization_barrier(jnp.max(scores, axis=-1, keepdims=True))
        weights = jnp.where(visible[None, None], jnp.exp(scores - highest), 0.0)
        totals = lax.optimization_barrier(jnp.sum(weights, axis=-1))
        rounded = lax.optimization_barrier(weights.astype(jnp.bfloat16)).astype(jnp.float32)
        mixed = jnp.einsum('kgrl,lkd->rkgd', rounded, value_rows, precision=lax.Precision.HIGHEST)
        mixed = mixed / totals.transpose(2, 0, 1)[..., None]
        results.append(mixed.reshape(ROWS, QH * HD).astype(jnp.bfloat16))
    return jnp.stack(results)

def section_update(heads_now, weight_now, rows_now):
    group_heads = QH // N_HEAD
    parts = heads_now.astype(jnp.float32).reshape(TICKS, ROWS, N_HEAD, group_heads * HD)
    weight_parts = weight_now.astype(jnp.float32).reshape(N_HEAD, group_heads * HD, D)
    results = []
    for tick_now in range(TICKS):
        partial_sums = jnp.einsum('rgk,gkd->grd', parts[tick_now], weight_parts, precision=lax.Precision.HIGHEST)
        rounded = lax.optimization_barrier(partial_sums.astype(jnp.bfloat16)).astype(jnp.float32)
        projected = lax.optimization_barrier(jnp.sum(rounded, axis=0))
        results.append((rows_now[:, tick_now].astype(jnp.float32) + projected).astype(jnp.bfloat16))
    return jnp.stack(results, axis=1)

def reference(residual, queries, new_kv, cache_kv, lengths, out_weight):
    query_sections = queries.reshape(TICKS, SECTIONS, ROWS, QH * HD).transpose(1, 0, 2, 3)
    fresh_sections = new_kv.reshape(TICKS, 2, SECTIONS, ROWS, KVH * HD).transpose(2, 0, 1, 3, 4)
    cache_sections = cache_kv.reshape(2, SECTIONS, CMAX, KVH * HD).transpose(1, 0, 2, 3)
    residual_sections = residual.reshape(SECTIONS, ROWS, TICKS, D)

    def per_section(items):
        query_now, fresh_now, cache_now, length_now, weight_now, rows_now = items
        heads_now = section_heads(query_now, fresh_now, cache_now, length_now)
        return section_update(heads_now, weight_now, rows_now)
    updated = lax.map(per_section, (query_sections, fresh_sections, cache_sections, lengths, out_weight, residual_sections))
    advanced = jnp.roll(updated, 1, axis=0)
    return advanced.reshape(TOKENS, TICKS, D)
```

```python
import functools
import math

import jax
import jax.numpy as jnp
from jax import lax
from jax.experimental import pallas as pl
from jax.experimental.pallas import tpu as pltpu
from jax.sharding import PartitionSpec as P

QH = 32
KVH = 8
HD = 128
GROUP = QH // KVH
KEY_BLOCK = 512
COLUMN_TILE = 512

neg_large = -1e30
EXPONENT = math.log2(math.e) / math.sqrt(HD)


def rows_kernel(
    ticks,
    rows,
    dep_count,
    place,
    queries,
    new_kv,
    cache_kv,
    out_weight,
    *rest,
):
    out = rest[dep_count]
    q_buf, fresh_buf, cache_buf, w_buf, heads_buf, acc_buf, in_sem, w_sem = rest[dep_count + 1 :]
    tick_count = len(ticks)
    fresh_count = ticks[-1] + 1
    row_first = pl.multiple_of(place[0], rows)
    my_length = place[1]
    kv_width = cache_buf.shape[2]
    kv_column = pl.multiple_of(place[2], HD)
    capacity = cache_buf.shape[1]
    fresh_rows = fresh_buf.shape[2]
    head_width = q_buf.shape[2]
    heads_here = head_width // HD
    kv_count = kv_width // HD
    inner = heads_here // kv_count
    tile_count = w_buf.shape[0]
    tile_width = w_buf.shape[2]

    copies = []
    for index, tick in enumerate(ticks):
        copies.append((queries.at[tick, pl.ds(row_first, rows), :], q_buf.at[index]))
    for tick in range(fresh_count):
        for part in range(2):
            copies.append(
                (new_kv.at[tick, part, :, pl.ds(kv_column, kv_width)], fresh_buf.at[tick, part])
            )
    for part in range(2):
        copies.append((cache_kv.at[part, :, pl.ds(kv_column, kv_width)], cache_buf.at[part]))
    started = [
        pltpu.make_async_copy(source, target, in_sem.at[index])
        for index, (source, target) in enumerate(copies)
    ]
    for copy in started:
        copy.start()
    w_copies = [
        pltpu.make_async_copy(
            out_weight.at[0, :, pl.ds(tile * tile_width, tile_width)], w_buf.at[tile], w_sem.at[tile]
        )
        for tile in range(tile_count)
    ]
    for copy in w_copies:
        copy.start()
    for copy in started:
        copy.wait()

    tick_rows = inner * rows
    all_rows = tick_count * tick_rows
    query_heads = []
    for g in range(kv_count):
        query_heads.append(
            jnp.concatenate(
                [
                    q_buf[index, :, (g * inner + i) * HD : (g * inner + i + 1) * HD]
                    for index in range(tick_count)
                    for i in range(inner)
                ],
                axis=0,
            )
        )

    def one_block(g, state, key_rows, value_rows, visible):
        highest, acc = state
        scores = lax.dot_general(
            query_heads[g], key_rows, (((1,), (1,)), ((), ())), preferred_element_type=jnp.float32
        )
        if visible is not None:
            scores = jnp.where(visible, scores, neg_large)
        now = jnp.maximum(highest, jnp.max(scores, axis=1, keepdims=True))
        weights = jnp.exp2((scores - now) * EXPONENT).astype(jnp.bfloat16)
        wide = jnp.concatenate([value_rows, jnp.ones_like(value_rows)], axis=1)
        added = jnp.dot(weights, wide, preferred_element_type=jnp.float32)
        if acc is not None:
            added = added + acc * jnp.exp2((highest - now) * EXPONENT)
        return now, added

    highest = []
    for g in range(kv_count):
        lanes = slice(g * HD, (g + 1) * HD)
        state = (jnp.full((all_rows, 1), neg_large, jnp.float32), None)
        for earlier in range(fresh_count):
            if tick_count == 1 and earlier < ticks[0]:
                visible = None
            else:
                shape = (all_rows, fresh_rows)
                line = lax.broadcasted_iota(jnp.int32, shape, 0)
                column = lax.broadcasted_iota(jnp.int32, shape, 1)
                position = lax.rem(line, rows) + row_first
                visible = column <= position
                if tick_count > 1:
                    tick_here = line // tick_rows + ticks[0]
                    visible = (tick_here > earlier) | ((tick_here == earlier) & visible)
            state = one_block(
                g,
                state,
                fresh_buf[earlier, 0, :, lanes],
                fresh_buf[earlier, 1, :, lanes],
                visible,
            )
        highest.append(state[0])
        acc_buf[g] = state[1]

    def cache_block(block, carry):
        start = pl.multiple_of(block * KEY_BLOCK, KEY_BLOCK)
        column = lax.broadcasted_iota(jnp.int32, (all_rows, KEY_BLOCK), 1)
        visible = column < my_length - start
        after = []
        for g in range(kv_count):
            lanes = slice(g * HD, (g + 1) * HD)
            now, acc = one_block(
                g,
                (carry[g], acc_buf[g]),
                cache_buf[0, pl.ds(start, KEY_BLOCK), lanes],
                cache_buf[1, pl.ds(start, KEY_BLOCK), lanes],
                visible,
            )
            acc_buf[g] = acc
            after.append(now)
        return tuple(after)

    lax.fori_loop(0, (my_length + KEY_BLOCK - 1) // KEY_BLOCK, cache_block, tuple(highest))

    for g in range(kv_count):
        mixed = (acc_buf[g, :, :HD] / acc_buf[g, :, HD:]).astype(jnp.bfloat16)
        for index in range(tick_count):
            for i in range(inner):
                head = g * inner + i
                first = (index * inner + i) * rows
                heads_buf[index * rows : (index + 1) * rows, head * HD : (head + 1) * HD] = mixed[
                    first : first + rows
                ]
    for tile in range(tile_count):
        w_copies[tile].wait()
        out[:, tile * tile_width : (tile + 1) * tile_width] = jnp.dot(
            heads_buf[...], w_buf[tile], preferred_element_type=jnp.float32
        ).astype(jnp.bfloat16)


def project_rows(ticks, rows, place, arrays, deps):
    queries, new_kv, cache_kv, out_weight = arrays
    head_width = queries.shape[2]
    heads_here = head_width // HD
    kv_count = max(1, heads_here // GROUP)
    kv_width = kv_count * HD
    capacity = cache_kv.shape[1]
    columns = out_weight.shape[2]
    tile = min(COLUMN_TILE, columns)
    fresh_count = ticks[-1] + 1
    tick_count = len(ticks)
    all_rows = tick_count * (heads_here // kv_count) * rows
    anywhere = pl.BlockSpec(memory_space=pl.ANY)
    return pl.pallas_call(
        functools.partial(rows_kernel, ticks, rows, len(deps)),
        out_shape=jax.ShapeDtypeStruct((tick_count * rows, columns), jnp.bfloat16),
        in_specs=[pl.BlockSpec(memory_space=pltpu.SMEM)] + [anywhere] * (4 + len(deps)),
        out_specs=pl.BlockSpec(memory_space=pltpu.VMEM),
        scratch_shapes=[
            pltpu.VMEM((tick_count, rows, head_width), jnp.bfloat16),
            pltpu.VMEM((fresh_count, 2, queries.shape[1], kv_width), jnp.bfloat16),
            pltpu.VMEM((2, capacity, kv_width), jnp.bfloat16),
            pltpu.VMEM((columns // tile, head_width, tile), jnp.bfloat16),
            pltpu.VMEM((tick_count * rows, head_width), jnp.bfloat16),
            pltpu.VMEM((kv_count, all_rows, 2 * HD), jnp.float32),
            pltpu.SemaphoreType.DMA((tick_count + 2 * fresh_count + 2,)),
            pltpu.SemaphoreType.DMA((columns // tile,)),
        ],
        compiler_params=pltpu.CompilerParams(vmem_limit_bytes=40 * 2**20),
        cost_estimate=pl.CostEstimate(flops=1000, bytes_accessed=1000, transcendentals=0),
    )(place, queries, new_kv, cache_kv, out_weight, *deps)


def add(left, right):
    return (left.astype(jnp.float32) + right.astype(jnp.float32)).astype(jnp.bfloat16)


def on_device(residual, queries, new_kv, cache_kv, lengths, out_weight):
    section_count = lax.axis_size("section")
    head_count = lax.axis_size("head")
    section_index = lax.axis_index("section")
    z = lax.axis_index("head")
    tick_count, row_count, head_width = queries.shape
    heads_here = head_width // HD
    kv_column = (z * heads_here // GROUP) * HD
    my_length = lengths[section_index]
    arrays = (queries, new_kv, cache_kv, out_weight)
    rows = row_count // head_count
    ticks = tuple(range(tick_count))

    def place(row_first):
        return jnp.stack([row_first, my_length, kv_column]).astype(jnp.int32)

    def send(block, pairs, distance):
        route = [
            (s * head_count + a, (s + distance) % section_count * head_count + b)
            for s in range(section_count)
            for a, b in pairs
        ]
        return lax.ppermute(block, ("section", "head"), route)

    def by_tick(block):
        return block.reshape(tick_count, -1, block.shape[-1])

    if head_count != 4 or tick_count != 2:
        partial = project_rows(ticks, row_count, place(0 * z), arrays, ())
        pieces = [
            lax.psum_scatter(block, "head", scatter_dimension=0, tiled=True)
            for block in by_tick(partial)
        ]
        updated = add(residual, jnp.stack(pieces, axis=1))
        return send(updated, [(i, i) for i in range(head_count)], 1)

    ends = [(0, 1), (3, 2)]
    middle = [(1, 2), (2, 1)]
    outward = [(0, 1), (3, 2), (1, 0), (2, 3)]
    same = [(i, i) for i in range(head_count)]
    lower = z < 2
    is_end = (z == 0) | (z == 3)
    first = jnp.where(lower, 3, 0)
    second = jnp.where(lower, 2, 1)
    third = jnp.where(is_end, jnp.where(lower, 1, 2), jnp.where(lower, 0, 3))

    def pieces_of(chunk, ticks_now, deps):
        return project_rows(ticks_now, rows, place(chunk * rows), arrays, deps)

    a0 = pieces_of(first, (0,), ())
    a1 = pieces_of(first, (1,), (a0,))
    b0 = pieces_of(second, (0,), (a1,))
    b1 = pieces_of(second, (1,), (b0,))
    a0_far = send(a0, ends, 0)
    a1_far = send(a1, ends, 0)
    b0_far = send(b0, ends, 0)
    b1_far = send(b1, ends, 0)
    a0_sum = add(a0, a0_far)
    a0_mid = send(a0_sum, middle, 0)
    own = pieces_of(z, ticks, (b1, a0_sum))
    base = add(by_tick(own), residual.transpose(1, 0, 2))
    base_here = send(base, same, 1)
    a1_sum = add(a1, a1_far)
    a1_mid = send(a1_sum, middle, 0)
    c = pieces_of(third, ticks, (own, a1_sum))
    c_here = send(add(by_tick(c), jnp.stack([a0_mid, a1_mid])), outward, 1)
    b0_here = send(add(b0, b0_far), middle, 1)
    b1_here = send(add(b1, b1_far), middle, 1)
    total = (
        base_here.astype(jnp.float32)
        + c_here.astype(jnp.float32)
        + jnp.stack([b0_here, b1_here]).astype(jnp.float32)
    )
    return total.astype(jnp.bfloat16).transpose(1, 0, 2)


def solution(mesh):
    placed = (
        P(("section", "head"), None, None),
        P(None, "section", "head"),
        P(None, None, "section", None),
        P(None, "section", None),
        P(),
        P("section", "head", None),
    )
    return jax.shard_map(
        on_device,
        mesh=mesh,
        in_specs=placed,
        out_specs=P(("section", "head"), None, None),
        check_vma=False,
    )
```

```python
import functools
import math

import jax
import jax.numpy as jnp
from jax import lax
from jax.experimental import pallas as pl
from jax.experimental.pallas import tpu as pltpu
from jax.sharding import PartitionSpec as P

QH = 32
KVH = 8
HD = 128
GROUP = QH // KVH
KEY_BLOCK = 512
WEIGHT_PARTS = 1
COLUMN_TILE = 1024

neg_large = -1e30
EXPONENT = math.log2(math.e) / math.sqrt(HD)


def scores_of(query_rows, key_rows):
    return lax.dot_general(
        query_rows, key_rows, (((1,), (1,)), ((), ())), preferred_element_type=jnp.float32
    )


def attend(ticks, rows, row_first, my_length, q_ref, fresh_ref, cache_ref, heads_ref):
    fresh_count = ticks[-1] + 1
    fresh_rows = fresh_ref.shape[2]
    capacity = cache_ref.shape[1]
    kv_count = fresh_ref.shape[3] // HD
    inner = q_ref.shape[2] // HD // kv_count
    key_block = min(KEY_BLOCK, capacity)
    tick_rows = inner * rows
    all_rows = len(ticks) * tick_rows

    def with_blocks(block_count):
        line = lax.broadcasted_iota(jnp.int32, (all_rows, fresh_rows), 0)
        position = lax.rem(line, rows) + row_first
        causal = lax.broadcasted_iota(jnp.int32, (all_rows, fresh_rows), 1) <= position
        for g in range(kv_count):
            lanes = slice(g * HD, (g + 1) * HD)
            query_rows = jnp.concatenate(
                [
                    q_ref[tick, pl.ds(row_first, rows), (g * inner + i) * HD : (g * inner + i + 1) * HD]
                    for tick in ticks
                    for i in range(inner)
                ],
                axis=0,
            )
            blocks = []
            for earlier in range(fresh_count):
                scores = scores_of(query_rows, fresh_ref[earlier, 0, :, lanes])
                if len(ticks) > 1:
                    tick_here = line // tick_rows + ticks[0]
                    seen = (tick_here > earlier) | ((tick_here == earlier) & causal)
                    scores = jnp.where(seen, scores, neg_large)
                elif earlier == ticks[0]:
                    scores = jnp.where(causal, scores, neg_large)
                blocks.append((scores, fresh_ref[earlier, 1, :, lanes]))
            for block in range(block_count):
                here = slice(block * key_block, (block + 1) * key_block)
                scores = scores_of(query_rows, cache_ref[0, here, lanes])
                if block == block_count - 1:
                    column = lax.broadcasted_iota(jnp.int32, scores.shape, 1)
                    scores = jnp.where(column < my_length - block * key_block, scores, neg_large)
                blocks.append((scores, cache_ref[1, here, lanes]))
            highest = None
            for scores, _ in blocks:
                for first in range(0, scores.shape[1], HD):
                    part = scores[:, first : first + HD]
                    highest = part if highest is None else jnp.maximum(highest, part)
            highest = jnp.max(highest, axis=1, keepdims=True)
            total = None
            for scores, values in blocks:
                weights = jnp.exp2((scores - highest) * EXPONENT).astype(jnp.bfloat16)
                wide = jnp.concatenate([values, jnp.ones_like(values)], axis=1)
                added = jnp.dot(weights, wide, preferred_element_type=jnp.float32)
                total = added if total is None else total + added
            mixed = (total[:, :HD] / total[:, HD:]).astype(jnp.bfloat16)
            for index in range(len(ticks)):
                for i in range(inner):
                    head = g * inner + i
                    first = (index * inner + i) * rows
                    heads_ref[
                        index * rows : (index + 1) * rows, head * HD : (head + 1) * HD
                    ] = mixed[first : first + rows]

    most = capacity // key_block
    used = (my_length + key_block - 1) // key_block
    for block_count in range(1, most + 1):

        @pl.when(used == block_count)
        def _():
            with_blocks(block_count)


def project(heads_ref, w_ref, outs):
    rows, columns = outs[0].shape
    tile = min(COLUMN_TILE, columns)
    for first in range(0, columns, tile):
        here = slice(first, first + tile)
        product = jnp.dot(heads_ref[...], w_ref[:, here], preferred_element_type=jnp.float32)
        for index, out in enumerate(outs):
            out[:, here] = product[index * rows : (index + 1) * rows].astype(out.dtype)


def load_kernel(
    ticks,
    rows,
    choose,
    lengths,
    queries,
    new_kv,
    cache_kv,
    out_weight,
    *rest,
):
    outs = rest[: len(ticks)]
    q_ref, fresh_ref, cache_ref, w_ref, heads_ref, sem = rest[len(ticks) :]
    z = lax.axis_index("head")
    kv_width = cache_ref.shape[2]
    heads_here = q_ref.shape[2] // HD
    kv_column = pl.multiple_of(z * heads_here // GROUP * HD, HD)
    lanes = pl.ds(kv_column, kv_width)
    pairs = [(queries, q_ref)]
    for tick in range(fresh_ref.shape[0]):
        for part in range(2):
            pairs.append((new_kv.at[tick, part, :, lanes], fresh_ref.at[tick, part]))
    for part in range(2):
        pairs.append((cache_kv.at[part, :, lanes], cache_ref.at[part]))
    part_rows = w_ref.shape[0] // WEIGHT_PARTS
    for part in range(WEIGHT_PARTS):
        here = pl.ds(part * part_rows, part_rows)
        pairs.append((out_weight.at[0, here, :], w_ref.at[here, :]))
    copies = [
        pltpu.make_async_copy(source, target, sem.at[index])
        for index, (source, target) in enumerate(pairs)
    ]
    for copy in copies:
        copy.start()
    for copy in copies[:-WEIGHT_PARTS]:
        copy.wait()
    row_first = pl.multiple_of(choose(z) * rows, rows)
    my_length = lengths[lax.axis_index("section")]
    attend(ticks, rows, row_first, my_length, q_ref, fresh_ref, cache_ref, heads_ref)
    for copy in copies[-WEIGHT_PARTS:]:
        copy.wait()
    project(heads_ref, w_ref, outs)


def rows_kernel(
    ticks, rows, choose, dep_count, lengths, q_ref, fresh_ref, cache_ref, w_ref, *rest
):
    outs = rest[dep_count : dep_count + len(ticks)]
    heads_ref = rest[-1]
    row_first = pl.multiple_of(choose(lax.axis_index("head")) * rows, rows)
    my_length = lengths[lax.axis_index("section")]
    attend(ticks, rows, row_first, my_length, q_ref, fresh_ref, cache_ref, heads_ref)
    project(heads_ref, w_ref, outs)


def in_vmem(array):
    return pltpu.with_memory_space_constraint(array, pltpu.VMEM)


def in_hbm(array):
    return pltpu.with_memory_space_constraint(array, pltpu.HBM)


WHOLE = pl.BlockSpec(memory_space=pltpu.VMEM)
ANYWHERE = pl.BlockSpec(memory_space=pl.ANY)
PARAMS = pltpu.CompilerParams(vmem_limit_bytes=28 * 2**20)
COST = pl.CostEstimate(flops=1000, bytes_accessed=1000, transcendentals=0)


def load_and_project(ticks, rows, choose, lengths, queries, new_kv, cache_kv, out_weight):
    tick_count, row_count, head_width = queries.shape
    kv_width = max(1, head_width // HD // GROUP) * HD
    columns = out_weight.shape[2]
    kind = queries.dtype
    piece = pltpu.VMEM((rows, columns), kind)
    out_shape = [piece] * len(ticks) + [
        pltpu.VMEM(queries.shape, kind),
        pltpu.VMEM((tick_count, 2, row_count, kv_width), kind),
        pltpu.VMEM((2, cache_kv.shape[1], kv_width), kind),
        pltpu.VMEM((head_width, columns), kind),
    ]
    results = pl.pallas_call(
        functools.partial(load_kernel, ticks, rows, choose),
        out_shape=out_shape,
        in_specs=[pl.BlockSpec(memory_space=pltpu.SMEM)] + [ANYWHERE] * 4,
        out_specs=[WHOLE] * len(out_shape),
        scratch_shapes=[
            pltpu.VMEM((len(ticks) * rows, head_width), kind),
            pltpu.SemaphoreType.DMA((3 + 2 * tick_count + WEIGHT_PARTS,)),
        ],
        compiler_params=PARAMS,
        cost_estimate=COST,
    )(lengths, *[in_hbm(array) for array in (queries, new_kv, cache_kv, out_weight)])
    return results[: len(ticks)], (lengths,) + tuple(results[len(ticks) :])


def project_rows(ticks, rows, choose, held, deps):
    lengths, queries, fresh, cache, weight = held
    columns = weight.shape[1]
    return pl.pallas_call(
        functools.partial(rows_kernel, ticks, rows, choose, len(deps)),
        out_shape=[pltpu.VMEM((rows, columns), queries.dtype)] * len(ticks),
        in_specs=[pl.BlockSpec(memory_space=pltpu.SMEM)] + [WHOLE] * 4 + [ANYWHERE] * len(deps),
        out_specs=[WHOLE] * len(ticks),
        scratch_shapes=[pltpu.VMEM((len(ticks) * rows, queries.shape[2]), queries.dtype)],
        compiler_params=PARAMS,
        cost_estimate=COST,
    )(lengths, *[in_vmem(array) for array in (queries, fresh, cache, weight)], *deps)


def add_kernel(count, *refs):
    out = refs[-1]
    for index in range(count):
        left, right = refs[index], refs[count + index]
        total = left[...].astype(jnp.float32) + right[...].astype(jnp.float32)
        if count == 1:
            out[...] = total.astype(out.dtype)
        else:
            out[index] = total.astype(out.dtype)


def add_after(left, right, deps):
    count = len(left)
    shape = left[0].shape if count == 1 else (count,) + left[0].shape
    return pl.pallas_call(
        functools.partial(add_kernel, count),
        out_shape=pltpu.VMEM(shape, left[0].dtype),
        in_specs=[WHOLE] * (2 * count) + [ANYWHERE] * len(deps),
        out_specs=WHOLE,
        compiler_params=PARAMS,
        cost_estimate=COST,
    )(*left, *right, *deps)


def add(left, right):
    return (left.astype(jnp.float32) + right.astype(jnp.float32)).astype(jnp.bfloat16)


def on_device(residual, queries, new_kv, cache_kv, lengths, out_weight):
    section_count = lax.axis_size("section")
    head_count = lax.axis_size("head")
    tick_count, row_count, head_width = queries.shape
    arrays = (lengths, queries, new_kv, cache_kv, out_weight)
    rows = row_count // head_count
    ticks = tuple(range(tick_count))

    def send(block, pairs, distance):
        route = [
            (s * head_count + a, (s + distance) % section_count * head_count + b)
            for s in range(section_count)
            for a, b in pairs
        ]
        return lax.ppermute(block, ("section", "head"), route)

    if head_count != 4 or tick_count != 2:
        partial, _ = load_and_project(ticks, row_count, lambda z: 0, *arrays)
        pieces = [
            lax.psum_scatter(block, "head", scatter_dimension=0, tiled=True) for block in partial
        ]
        updated = add(residual, jnp.stack(pieces, axis=1))
        return send(updated, [(i, i) for i in range(head_count)], 1)

    ends = [(0, 1), (3, 2)]
    middle = [(1, 2), (2, 1)]
    outward = [(0, 1), (3, 2), (1, 0), (2, 3)]
    same = [(i, i) for i in range(head_count)]

    def first(z):
        return jnp.where(z < 2, 3, 0)

    def second(z):
        return jnp.where(z < 2, 2, 1)

    def third(z):
        return jnp.where(z == 0, 1, jnp.where(z == 1, 0, jnp.where(z == 2, 3, 2)))

    (a0,), held = load_and_project((0,), rows, first, *arrays)
    a0_far = send(a0, ends, 0)
    (a1,) = project_rows((1,), rows, first, held, (a0,))
    a1_far = send(a1, ends, 0)
    b0, b1 = project_rows(ticks, rows, second, held, (a1,))
    b0_far = send(b0, ends, 0)
    b1_far = send(b1, ends, 0)
    a0_sum = add_after([a0], [a0_far], (b0,))
    a0_mid = send(a0_sum, middle, 0)
    own = project_rows(ticks, rows, lambda z: z, held, (a0_sum,))
    base = add(jnp.stack(own), residual.transpose(1, 0, 2))
    base_here = send(base, same, 1)
    a1_sum = add_after([a1], [a1_far], (own[0],))
    a1_mid = send(a1_sum, middle, 0)
    c = project_rows(ticks, rows, third, held, (a1_sum,))
    b0_sum = add_after([b0], [b0_far], (c[0],))
    b0_here = send(b0_sum, middle, 1)
    c_sum = add_after(c, [a0_mid, a1_mid], (b0_sum,))
    c_here = send(c_sum, outward, 1)
    b1_sum = add_after([b1], [b1_far], (c_sum, base_here))
    b1_here = send(b1_sum, middle, 1)
    total = (
        base_here.astype(jnp.float32)
        + c_here.astype(jnp.float32)
        + jnp.stack([b0_here, b1_here]).astype(jnp.float32)
    )
    return total.astype(jnp.bfloat16).transpose(1, 0, 2)


def solution(mesh):
    placed = (
        P(("section", "head"), None, None),
        P(None, "section", "head"),
        P(None, None, "section", None),
        P(None, "section", None),
        P(),
        P("section", "head", None),
    )
    return jax.shard_map(
        on_device,
        mesh=mesh,
        in_specs=placed,
        out_specs=P(("section", "head"), None, None),
        check_vma=False,
    )
```

```python
import functools
import math

import jax
import jax.numpy as jnp
from jax import lax
from jax.experimental import pallas as pl
from jax.experimental.pallas import tpu as pltpu
from jax.sharding import PartitionSpec as P

QH = 32
KVH = 8
HD = 128
GROUP = QH // KVH
KEY_BLOCK = 512
WEIGHT_PARTS = 1
COLUMN_TILE = 1024

neg_large = -1e30
EXPONENT = math.log2(math.e) / math.sqrt(HD)


def scores_of(query_rows, key_rows):
    return lax.dot_general(
        query_rows, key_rows, (((1,), (1,)), ((), ())), preferred_element_type=jnp.float32
    )


def attend(ticks, rows, row_first, my_length, q_ref, fresh_ref, cache_ref, heads_ref):
    fresh_count = ticks[-1] + 1
    fresh_rows = fresh_ref.shape[2]
    capacity = cache_ref.shape[1]
    kv_count = fresh_ref.shape[3] // HD
    inner = q_ref.shape[2] // HD // kv_count
    key_block = min(KEY_BLOCK, capacity)
    tick_rows = inner * rows
    all_rows = len(ticks) * tick_rows

    line = lax.broadcasted_iota(jnp.int32, (all_rows, fresh_rows), 0)
    position = lax.rem(line, rows) + row_first
    causal = lax.broadcasted_iota(jnp.int32, (all_rows, fresh_rows), 1) <= position
    for g in range(kv_count):
        lanes = slice(g * HD, (g + 1) * HD)
        query_rows = jnp.concatenate(
            [
                q_ref[tick, pl.ds(row_first, rows), (g * inner + i) * HD : (g * inner + i + 1) * HD]
                for tick in ticks
                for i in range(inner)
            ],
            axis=0,
        )
        blocks = []
        for earlier in range(fresh_count):
            scores = scores_of(query_rows, fresh_ref[earlier, 0, :, lanes])
            if len(ticks) > 1:
                tick_here = line // tick_rows + ticks[0]
                seen = (tick_here > earlier) | ((tick_here == earlier) & causal)
                scores = jnp.where(seen, scores, neg_large)
            elif earlier == ticks[0]:
                scores = jnp.where(causal, scores, neg_large)
            blocks.append((scores, fresh_ref[earlier, 1, :, lanes]))
        for block in range(capacity // key_block):
            here = slice(block * key_block, (block + 1) * key_block)
            scores = scores_of(query_rows, cache_ref[0, here, lanes])
            column = lax.broadcasted_iota(jnp.int32, scores.shape, 1)
            scores = jnp.where(column < my_length - block * key_block, scores, neg_large)
            blocks.append((scores, cache_ref[1, here, lanes]))
        highest = None
        for scores, _ in blocks:
            for first in range(0, scores.shape[1], HD):
                part = scores[:, first : first + HD]
                highest = part if highest is None else jnp.maximum(highest, part)
        highest = jnp.max(highest, axis=1, keepdims=True)
        total = None
        for scores, values in blocks:
            weights = jnp.exp2((scores - highest) * EXPONENT).astype(jnp.bfloat16)
            wide = jnp.concatenate([values, jnp.ones_like(values)], axis=1)
            added = jnp.dot(weights, wide, preferred_element_type=jnp.float32)
            total = added if total is None else total + added
        mixed = (total[:, :HD] / total[:, HD:]).astype(jnp.bfloat16)
        for index in range(len(ticks)):
            for i in range(inner):
                head = g * inner + i
                first = (index * inner + i) * rows
                heads_ref[
                    index * rows : (index + 1) * rows, head * HD : (head + 1) * HD
                ] = mixed[first : first + rows]


def project(heads_ref, w_ref, outs):
    rows, columns = outs[0].shape
    tile = min(COLUMN_TILE, columns)
    for first in range(0, columns, tile):
        here = slice(first, first + tile)
        product = jnp.dot(heads_ref[...], w_ref[:, here], preferred_element_type=jnp.float32)
        for index, out in enumerate(outs):
            out[:, here] = product[index * rows : (index + 1) * rows].astype(out.dtype)


def load_kernel(
    ticks,
    rows,
    choose,
    lengths,
    queries,
    new_kv,
    cache_kv,
    out_weight,
    *rest,
):
    outs = rest[: len(ticks)]
    q_ref, fresh_ref, cache_ref, w_ref, heads_ref, sem = rest[len(ticks) :]
    z = lax.axis_index("head")
    kv_width = cache_ref.shape[2]
    heads_here = q_ref.shape[2] // HD
    kv_column = pl.multiple_of(z * heads_here // GROUP * HD, HD)
    lanes = pl.ds(kv_column, kv_width)
    pairs = [(queries, q_ref)]
    for tick in range(fresh_ref.shape[0]):
        for part in range(2):
            pairs.append((new_kv.at[tick, part, :, lanes], fresh_ref.at[tick, part]))
    for part in range(2):
        pairs.append((cache_kv.at[part, :, lanes], cache_ref.at[part]))
    part_rows = w_ref.shape[0] // WEIGHT_PARTS
    for part in range(WEIGHT_PARTS):
        here = pl.ds(part * part_rows, part_rows)
        pairs.append((out_weight.at[0, here, :], w_ref.at[here, :]))
    copies = [
        pltpu.make_async_copy(source, target, sem.at[index])
        for index, (source, target) in enumerate(pairs)
    ]
    for copy in copies:
        copy.start()
    for copy in copies[:-WEIGHT_PARTS]:
        copy.wait()
    row_first = pl.multiple_of(choose(z) * rows, rows)
    my_length = lengths[lax.axis_index("section")]
    attend(ticks, rows, row_first, my_length, q_ref, fresh_ref, cache_ref, heads_ref)
    for copy in copies[-WEIGHT_PARTS:]:
        copy.wait()
    project(heads_ref, w_ref, outs)


def rows_kernel(
    ticks, rows, choose, dep_count, lengths, q_ref, fresh_ref, cache_ref, w_ref, *rest
):
    outs = rest[dep_count : dep_count + len(ticks)]
    heads_ref = rest[-1]
    row_first = pl.multiple_of(choose(lax.axis_index("head")) * rows, rows)
    my_length = lengths[lax.axis_index("section")]
    attend(ticks, rows, row_first, my_length, q_ref, fresh_ref, cache_ref, heads_ref)
    project(heads_ref, w_ref, outs)


def in_vmem(array):
    return pltpu.with_memory_space_constraint(array, pltpu.VMEM)


def in_hbm(array):
    return pltpu.with_memory_space_constraint(array, pltpu.HBM)


WHOLE = pl.BlockSpec(memory_space=pltpu.VMEM)
ANYWHERE = pl.BlockSpec(memory_space=pl.ANY)
PARAMS = pltpu.CompilerParams(vmem_limit_bytes=28 * 2**20)
COST = pl.CostEstimate(flops=1000, bytes_accessed=1000, transcendentals=0)


def load_and_project(ticks, rows, choose, lengths, queries, new_kv, cache_kv, out_weight):
    tick_count, row_count, head_width = queries.shape
    kv_width = max(1, head_width // HD // GROUP) * HD
    columns = out_weight.shape[2]
    kind = queries.dtype
    piece = pltpu.VMEM((rows, columns), kind)
    out_shape = [piece] * len(ticks) + [
        pltpu.VMEM(queries.shape, kind),
        pltpu.VMEM((tick_count, 2, row_count, kv_width), kind),
        pltpu.VMEM((2, cache_kv.shape[1], kv_width), kind),
        pltpu.VMEM((head_width, columns), kind),
    ]
    results = pl.pallas_call(
        functools.partial(load_kernel, ticks, rows, choose),
        out_shape=out_shape,
        in_specs=[pl.BlockSpec(memory_space=pltpu.SMEM)] + [ANYWHERE] * 4,
        out_specs=[WHOLE] * len(out_shape),
        scratch_shapes=[
            pltpu.VMEM((len(ticks) * rows, head_width), kind),
            pltpu.SemaphoreType.DMA((3 + 2 * tick_count + WEIGHT_PARTS,)),
        ],
        compiler_params=PARAMS,
        cost_estimate=COST,
    )(lengths, *[in_hbm(array) for array in (queries, new_kv, cache_kv, out_weight)])
    return results[: len(ticks)], (lengths,) + tuple(results[len(ticks) :])


def project_rows(ticks, rows, choose, held, deps):
    lengths, queries, fresh, cache, weight = held
    columns = weight.shape[1]
    return pl.pallas_call(
        functools.partial(rows_kernel, ticks, rows, choose, len(deps)),
        out_shape=[pltpu.VMEM((rows, columns), queries.dtype)] * len(ticks),
        in_specs=[pl.BlockSpec(memory_space=pltpu.SMEM)] + [WHOLE] * 4 + [ANYWHERE] * len(deps),
        out_specs=[WHOLE] * len(ticks),
        scratch_shapes=[pltpu.VMEM((len(ticks) * rows, queries.shape[2]), queries.dtype)],
        compiler_params=PARAMS,
        cost_estimate=COST,
    )(lengths, *[in_vmem(array) for array in (queries, fresh, cache, weight)], *deps)


def add_kernel(count, *refs):
    out = refs[-1]
    for index in range(count):
        left, right = refs[index], refs[count + index]
        total = left[...].astype(jnp.float32) + right[...].astype(jnp.float32)
        if count == 1:
            out[...] = total.astype(out.dtype)
        else:
            out[index] = total.astype(out.dtype)


def add_after(left, right, deps):
    count = len(left)
    shape = left[0].shape if count == 1 else (count,) + left[0].shape
    return pl.pallas_call(
        functools.partial(add_kernel, count),
        out_shape=pltpu.VMEM(shape, left[0].dtype),
        in_specs=[WHOLE] * (2 * count) + [ANYWHERE] * len(deps),
        out_specs=WHOLE,
        compiler_params=PARAMS,
        cost_estimate=COST,
    )(*left, *right, *deps)


def add(left, right):
    return (left.astype(jnp.float32) + right.astype(jnp.float32)).astype(jnp.bfloat16)


def on_device(residual, queries, new_kv, cache_kv, lengths, out_weight):
    section_count = lax.axis_size("section")
    head_count = lax.axis_size("head")
    tick_count, row_count, head_width = queries.shape
    arrays = (lengths, queries, new_kv, cache_kv, out_weight)
    rows = row_count // head_count
    ticks = tuple(range(tick_count))

    def send(block, pairs, distance):
        route = [
            (s * head_count + a, (s + distance) % section_count * head_count + b)
            for s in range(section_count)
            for a, b in pairs
        ]
        return lax.ppermute(block, ("section", "head"), route)

    if head_count != 4 or tick_count != 2:
        partial, _ = load_and_project(ticks, row_count, lambda z: 0, *arrays)
        pieces = [
            lax.psum_scatter(block, "head", scatter_dimension=0, tiled=True) for block in partial
        ]
        updated = add(residual, jnp.stack(pieces, axis=1))
        return send(updated, [(i, i) for i in range(head_count)], 1)

    ends = [(0, 1), (3, 2)]
    middle = [(1, 2), (2, 1)]
    outward = [(0, 1), (3, 2), (1, 0), (2, 3)]
    same = [(i, i) for i in range(head_count)]

    def first(z):
        return jnp.where(z < 2, 3, 0)

    def second(z):
        return jnp.where(z < 2, 2, 1)

    def third(z):
        return jnp.where(z == 0, 1, jnp.where(z == 1, 0, jnp.where(z == 2, 3, 2)))

    (a0,), held = load_and_project((0,), rows, first, *arrays)
    a0_far = send(a0, ends, 0)
    (a1,) = project_rows((1,), rows, first, held, (a0,))
    a1_far = send(a1, ends, 0)
    b0, b1 = project_rows(ticks, rows, second, held, (a1,))
    b0_far = send(b0, ends, 0)
    b1_far = send(b1, ends, 0)
    a0_sum = add_after([a0], [a0_far], (b0,))
    a0_mid = send(a0_sum, middle, 0)
    own = project_rows(ticks, rows, lambda z: z, held, (a0_sum,))
    base = add(jnp.stack(own), residual.transpose(1, 0, 2))
    base_here = send(base, same, 1)
    a1_sum = add_after([a1], [a1_far], (own[0],))
    a1_mid = send(a1_sum, middle, 0)
    c = project_rows(ticks, rows, third, held, (a1_sum,))
    b0_sum = add_after([b0], [b0_far], (c[0],))
    b0_here = send(b0_sum, middle, 1)
    c_sum = add_after(c, [a0_mid, a1_mid], (b0_sum,))
    c_here = send(c_sum, outward, 1)
    b1_sum = add_after([b1], [b1_far], (c_sum, base_here))
    b1_here = send(b1_sum, middle, 1)
    total = (
        base_here.astype(jnp.float32)
        + c_here.astype(jnp.float32)
        + jnp.stack([b0_here, b1_here]).astype(jnp.float32)
    )
    return total.astype(jnp.bfloat16).transpose(1, 0, 2)


def solution(mesh):
    placed = (
        P(("section", "head"), None, None),
        P(None, "section", "head"),
        P(None, None, "section", None),
        P(None, "section", None),
        P(),
        P("section", "head", None),
    )
    return jax.shard_map(
        on_device,
        mesh=mesh,
        in_specs=placed,
        out_specs=P(("section", "head"), None, None),
        check_vma=False,
    )
```

```python
import functools
import math

import jax
import jax.numpy as jnp
from jax import lax
from jax.experimental import pallas as pl
from jax.experimental.pallas import tpu as pltpu
from jax.sharding import PartitionSpec as P

QH = 32
KVH = 8
HD = 128
GROUP = QH // KVH
KEY_BLOCK = 512
WEIGHT_PARTS = 4
COLUMN_TILE = 1024

neg_large = -1e30
EXPONENT = math.log2(math.e) / math.sqrt(HD)


def scores_of(query_rows, key_rows):
    return lax.dot_general(
        query_rows, key_rows, (((1,), (1,)), ((), ())), preferred_element_type=jnp.float32
    )


def attend(ticks, rows, row_first, my_length, query_of, fresh_ref, cache_ref, heads_ref):
    fresh_count = ticks[-1] + 1
    fresh_rows = fresh_ref.shape[2]
    capacity = cache_ref.shape[1]
    kv_count = fresh_ref.shape[3] // HD
    inner = heads_ref.shape[1] // HD // kv_count
    key_block = min(KEY_BLOCK, capacity)
    tick_rows = inner * rows
    all_rows = len(ticks) * tick_rows
    line = lax.broadcasted_iota(jnp.int32, (all_rows, fresh_rows), 0)
    position = lax.rem(line, rows) + row_first
    causal = lax.broadcasted_iota(jnp.int32, (all_rows, fresh_rows), 1) <= position
    for g in range(kv_count):
        lanes = slice(g * HD, (g + 1) * HD)
        query_rows = jnp.concatenate(
            [
                query_of(index, slice((g * inner + i) * HD, (g * inner + i + 1) * HD))
                for index in range(len(ticks))
                for i in range(inner)
            ],
            axis=0,
        )
        blocks = []
        for earlier in range(fresh_count):
            scores = scores_of(query_rows, fresh_ref[earlier, 0, :, lanes])
            if len(ticks) > 1:
                tick_here = line // tick_rows + ticks[0]
                seen = (tick_here > earlier) | ((tick_here == earlier) & causal)
                scores = jnp.where(seen, scores, neg_large)
            elif earlier == ticks[0]:
                scores = jnp.where(causal, scores, neg_large)
            blocks.append((scores, fresh_ref[earlier, 1, :, lanes]))
        for block in range(capacity // key_block):
            here = slice(block * key_block, (block + 1) * key_block)
            scores = scores_of(query_rows, cache_ref[0, here, lanes])
            column = lax.broadcasted_iota(jnp.int32, scores.shape, 1)
            scores = jnp.where(column < my_length - block * key_block, scores, neg_large)
            blocks.append((scores, cache_ref[1, here, lanes]))
        highest = None
        for scores, _ in blocks:
            for first in range(0, scores.shape[1], HD):
                part = scores[:, first : first + HD]
                highest = part if highest is None else jnp.maximum(highest, part)
        highest = jnp.max(highest, axis=1, keepdims=True)
        total = None
        for scores, values in blocks:
            weights = jnp.exp2((scores - highest) * EXPONENT).astype(jnp.bfloat16)
            wide = jnp.concatenate([values, jnp.ones_like(values)], axis=1)
            added = jnp.dot(weights, wide, preferred_element_type=jnp.float32)
            total = added if total is None else total + added
        mixed = (total[:, :HD] / total[:, HD:]).astype(jnp.bfloat16)
        for index in range(len(ticks)):
            for i in range(inner):
                head = g * inner + i
                first = (index * inner + i) * rows
                heads_ref[
                    index * rows : (index + 1) * rows, head * HD : (head + 1) * HD
                ] = mixed[first : first + rows]


def project(heads_ref, w_ref, outs):
    rows, columns = outs[0].shape
    tile = min(COLUMN_TILE, columns)
    for first in range(0, columns, tile):
        here = slice(first, first + tile)
        product = jnp.dot(heads_ref[...], w_ref[:, here], preferred_element_type=jnp.float32)
        for index, out in enumerate(outs):
            out[:, here] = product[index * rows : (index + 1) * rows].astype(out.dtype)


def project_arriving(heads_ref, w_ref, outs, sum_ref, copies):
    rows, columns = outs[0].shape
    tile = min(COLUMN_TILE, columns)
    part_rows = w_ref.shape[0] // len(copies)
    for part, copy in enumerate(copies):
        copy.wait()
        depth = slice(part * part_rows, (part + 1) * part_rows)
        for first in range(0, columns, tile):
            here = slice(first, first + tile)
            product = jnp.dot(
                heads_ref[:, depth], w_ref[depth, here], preferred_element_type=jnp.float32
            )
            if part > 0:
                product = product + sum_ref[:, here]
            if part < len(copies) - 1:
                sum_ref[:, here] = product
            else:
                for index, out in enumerate(outs):
                    out[:, here] = product[index * rows : (index + 1) * rows].astype(out.dtype)


def held_copies(new_kv, cache_kv, out_weight, fresh_ref, cache_ref, w_ref, sem):
    kv_width = cache_ref.shape[2]
    heads_here = w_ref.shape[0] // HD
    kv_column = pl.multiple_of(lax.axis_index("head") * heads_here // GROUP * HD, HD)
    lanes = pl.ds(kv_column, kv_width)
    pairs = []
    for tick in range(fresh_ref.shape[0]):
        for part in range(2):
            pairs.append((new_kv.at[tick, part, :, lanes], fresh_ref.at[tick, part]))
    for part in range(2):
        pairs.append((cache_kv.at[part, :, lanes], cache_ref.at[part]))
    part_rows = w_ref.shape[0] // WEIGHT_PARTS
    for part in range(WEIGHT_PARTS):
        here = pl.ds(part * part_rows, part_rows)
        pairs.append((out_weight.at[0, here, :], w_ref.at[here, :]))
    copies = [
        pltpu.make_async_copy(source, target, sem.at[index])
        for index, (source, target) in enumerate(pairs)
    ]
    return copies[:-WEIGHT_PARTS], copies[-WEIGHT_PARTS:]


def first_kernel(
    ticks, rows, choose, active, lengths, queries, new_kv, cache_kv, out_weight, *rest
):
    outs = rest[: len(ticks)]
    fresh_ref, cache_ref, w_ref, length_ref, q_ref, heads_ref, sum_ref, sem = rest[len(ticks) :]
    z = lax.axis_index("head")

    @pl.when(active(z))
    def _():
        row_first = pl.multiple_of(choose(z) * rows, rows)
        copies, w_copies = held_copies(
            new_kv, cache_kv, out_weight, fresh_ref, cache_ref, w_ref, sem
        )
        used = len(copies) + len(w_copies)
        copies.append(pltpu.make_async_copy(lengths, length_ref, sem.at[used]))
        for index, tick in enumerate(ticks):
            copies.append(
                pltpu.make_async_copy(
                    queries.at[tick, pl.ds(row_first, rows), :],
                    q_ref.at[index],
                    sem.at[used + 1 + index],
                )
            )
        for copy in copies + w_copies:
            copy.start()
        for copy in copies:
            copy.wait()
        attend(
            ticks,
            rows,
            row_first,
            length_ref[lax.axis_index("section")],
            lambda index, lanes: q_ref[index, :, lanes],
            fresh_ref,
            cache_ref,
            heads_ref,
        )
        project_arriving(heads_ref, w_ref, outs, sum_ref, w_copies)


def later_rows(ticks, rows, choose, lengths, q_ref, fresh_ref, cache_ref, heads_ref):
    row_first = pl.multiple_of(choose(lax.axis_index("head")) * rows, rows)
    attend(
        ticks,
        rows,
        row_first,
        lengths[lax.axis_index("section")],
        lambda index, lanes: q_ref[ticks[index], pl.ds(row_first, rows), lanes],
        fresh_ref,
        cache_ref,
        heads_ref,
    )


def second_kernel(
    ticks,
    rows,
    choose,
    active,
    lengths,
    queries,
    new_kv,
    cache_kv,
    out_weight,
    residual,
    fresh_in,
    cache_in,
    w_in,
    dep,
    *rest,
):
    outs = rest[: len(ticks)]
    q_ref, by_tick_ref, fresh_ref, cache_ref, w_ref, *scratch = rest[len(ticks) :]
    heads_ref, residual_ref, sem, q_sem, residual_sem = scratch
    late = jnp.logical_not(active(lax.axis_index("head")))
    copies, w_copies = held_copies(new_kv, cache_kv, out_weight, fresh_ref, cache_ref, w_ref, sem)
    q_copy = pltpu.make_async_copy(queries, q_ref, q_sem)
    q_copy.start()
    residual_copy = pltpu.make_async_copy(residual, residual_ref, residual_sem)
    residual_copy.start()

    @pl.when(late)
    def _():
        for copy in copies + w_copies:
            copy.start()
        for copy in copies:
            copy.wait()

    q_copy.wait()
    later_rows(ticks, rows, choose, lengths, q_ref, fresh_ref, cache_ref, heads_ref)

    @pl.when(late)
    def _():
        for copy in w_copies:
            copy.wait()

    project(heads_ref, w_ref, outs)
    residual_copy.wait()
    for tick in range(by_tick_ref.shape[0]):
        by_tick_ref[tick] = residual_ref[:, tick, :]


def plus(left, right, out):
    out[...] = (left[...].astype(jnp.float32) + right[...].astype(jnp.float32)).astype(out.dtype)


def rows_kernel(ticks, rows, choose, active, names, *refs):
    ref = dict(zip(names, refs))
    if "out" in ref:
        outs = [ref["out"].at[index] for index in range(len(ticks))]
    else:
        outs = [ref["out%d" % index] for index in range(len(ticks))]

    @pl.when(active(lax.axis_index("head")))
    def _():
        later_rows(
            ticks, rows, choose, ref["lengths"], ref["q"], ref["fresh"], ref["cache"], ref["heads"]
        )
        project(ref["heads"], ref["w"], outs)
        if "residual" in ref:
            for index, out in enumerate(outs):
                plus(out, ref["residual"].at[index], out)


def in_vmem(array):
    return pltpu.with_memory_space_constraint(array, pltpu.VMEM)


def in_hbm(array):
    return pltpu.with_memory_space_constraint(array, pltpu.HBM)


WHOLE = pl.BlockSpec(memory_space=pltpu.VMEM)
ANYWHERE = pl.BlockSpec(memory_space=pl.ANY)
PARAMS = pltpu.CompilerParams(vmem_limit_bytes=28 * 2**20)
def cost_of(flops):
    return pl.CostEstimate(flops=flops, bytes_accessed=1000, transcendentals=0)


COST = cost_of(1000)
COST_OWN = cost_of(4 * 10**9)
COST_SUM = cost_of(4500 * 10**6)
COST_D = cost_of(4500 * 10**6)
COST_C = cost_of(4500 * 10**6)
LONG = cost_of(4 * 10**10)


def held_shapes(queries, new_kv, cache_kv, out_weight):
    tick_count, row_count, head_width = queries.shape
    kv_width = max(1, head_width // HD // GROUP) * HD
    kind = queries.dtype
    return [
        pltpu.VMEM((tick_count, 2, row_count, kv_width), kind),
        pltpu.VMEM((2, cache_kv.shape[1], kv_width), kind),
        pltpu.VMEM((head_width, out_weight.shape[2]), kind),
    ]


def first_rows(ticks, rows, choose, active, lengths, *arrays):
    queries, out_weight = arrays[0], arrays[3]
    tick_count, row_count, head_width = queries.shape
    columns = out_weight.shape[2]
    kind = queries.dtype
    out_shape = [pltpu.VMEM((rows, columns), kind)] * len(ticks) + held_shapes(*arrays)
    results = pl.pallas_call(
        functools.partial(first_kernel, ticks, rows, choose, active),
        out_shape=out_shape,
        in_specs=[ANYWHERE] * 5,
        out_specs=[WHOLE] * len(out_shape),
        scratch_shapes=[
            pltpu.SMEM(lengths.shape, lengths.dtype),
            pltpu.VMEM((len(ticks), rows, head_width), kind),
            pltpu.VMEM((len(ticks) * rows, head_width), kind),
            pltpu.VMEM((len(ticks) * rows, columns), jnp.float32),
            pltpu.SemaphoreType.DMA((3 + 2 * tick_count + WEIGHT_PARTS + len(ticks),)),
        ],
        compiler_params=PARAMS,
        cost_estimate=COST,
    )(*[in_hbm(array) for array in (lengths, *arrays)])
    return results[: len(ticks)], results[len(ticks) :]


def second_rows(ticks, rows, choose, active, lengths, arrays, residual, held, dep):
    queries, out_weight = arrays[0], arrays[3]
    tick_count, row_count, head_width = queries.shape
    kind = queries.dtype
    out_shape = [pltpu.VMEM((rows, out_weight.shape[2]), kind)] * len(ticks)
    out_shape += [
        pltpu.VMEM(queries.shape, kind),
        pltpu.VMEM((tick_count, residual.shape[0], residual.shape[2]), kind),
    ] + held_shapes(*arrays)
    results = pl.pallas_call(
        functools.partial(second_kernel, ticks, rows, choose, active),
        out_shape=out_shape,
        in_specs=[pl.BlockSpec(memory_space=pltpu.SMEM)] + [ANYWHERE] * 5 + [WHOLE] * 3 + [ANYWHERE],
        out_specs=[WHOLE] * len(out_shape),
        scratch_shapes=[
            pltpu.VMEM((len(ticks) * rows, head_width), kind),
            pltpu.VMEM(residual.shape, kind),
            pltpu.SemaphoreType.DMA((2 + 2 * tick_count + WEIGHT_PARTS,)),
            pltpu.SemaphoreType.DMA,
            pltpu.SemaphoreType.DMA,
        ],
        input_output_aliases={6 + index: len(ticks) + 2 + index for index in range(3)},
        compiler_params=PARAMS,
        cost_estimate=COST,
    )(
        lengths,
        *[in_hbm(array) for array in (*arrays, residual)],
        *[in_vmem(array) for array in held],
        dep,
    )
    here = len(ticks)
    return results[:here], results[here + 1], (lengths, results[here], *results[here + 2 :])


def project_rows(ticks, rows, choose, active, held, blocks, cost, deps, split=False):
    lengths, queries, fresh, cache, weight = held
    columns = weight.shape[1]
    kind = queries.dtype
    operands = {"q": queries, "fresh": fresh, "cache": cache, "w": weight}
    operands.update(blocks)
    if split:
        outs = {"out%d" % index: pltpu.VMEM((rows, columns), kind) for index in range(len(ticks))}
    else:
        outs = {"out": pltpu.VMEM((len(ticks), rows, columns), kind)}
    names = ["lengths"] + list(operands) + ["dep"] * len(deps) + list(outs) + ["heads"]
    return pl.pallas_call(
        functools.partial(rows_kernel, ticks, rows, choose, active, names),
        out_shape=list(outs.values()),
        in_specs=[pl.BlockSpec(memory_space=pltpu.SMEM)]
        + [WHOLE] * len(operands)
        + [ANYWHERE] * len(deps),
        out_specs=[WHOLE] * len(outs),
        scratch_shapes=[pltpu.VMEM((len(ticks) * rows, queries.shape[2]), kind)],
        compiler_params=PARAMS,
        cost_estimate=cost,
    )(lengths, *[in_vmem(array) for array in operands.values()], *deps)


def small_kernel(kernel, shape, kind, cost, *blocks, deps=()):
    return pl.pallas_call(
        kernel,
        out_shape=pltpu.VMEM(shape, kind),
        in_specs=[WHOLE] * len(blocks) + [ANYWHERE] * len(deps),
        out_specs=WHOLE,
        compiler_params=PARAMS,
        cost_estimate=cost,
    )(*blocks, *deps)


def add_kernel(left, right, *rest):
    plus(left, right, rest[-1])


def by_role_kernel(active, count, *refs):
    out = refs[-1]
    plain, left, right = refs[:count], refs[count : 2 * count], refs[2 * count : 3 * count]
    here = active(lax.axis_index("head"))

    @pl.when(here)
    def _():
        for index in range(count):
            plus(left[index], right[index], out.at[index])

    @pl.when(jnp.logical_not(here))
    def _():
        for index in range(count):
            out[index] = plain[index][...]


def whole_or_parts(refs, ticks):
    return [refs[0].at[index] for index in range(ticks)] if len(refs) == 1 else list(refs)


def outward_kernel(active, ticks, plain, left, *rest):
    refs = whole_or_parts([plain], ticks) + whole_or_parts([left], ticks) + list(rest[:ticks])
    by_role_kernel(active, ticks, *refs, rest[-1])


def inner_kernel(active, ticks, *refs):
    plain = list(refs[:ticks])
    left, right = refs[ticks], refs[ticks + 1]
    refs = plain + whole_or_parts([left], ticks) + whole_or_parts([right], ticks) + [refs[-1]]
    by_role_kernel(active, ticks, *refs)


def add_wide_kernel(ticks, block, *refs):
    out = refs[-1]
    for index in range(ticks):
        out[index] = block[index].astype(jnp.float32) + refs[index][...].astype(jnp.float32)


def finish_kernel(wide, block, out, buf, sem):
    step = 16
    copies = []
    for first in range(0, out.shape[0], step):
        here = pl.ds(first, step)
        for tick in range(out.shape[1]):
            total = wide[tick, here, :] + block[tick, here, :].astype(jnp.float32)
            buf[here, tick, :] = total.astype(out.dtype)
        copies.append(pltpu.make_async_copy(buf.at[here], out.at[here], sem.at[first // step]))
        copies[-1].start()
    for copy in copies:
        copy.wait()


def finish(wide, block):
    tick_count, rows, columns = block.shape
    shape = (rows, tick_count, columns)
    return pl.pallas_call(
        finish_kernel,
        out_shape=jax.ShapeDtypeStruct(shape, block.dtype),
        in_specs=[WHOLE] * 2,
        out_specs=ANYWHERE,
        scratch_shapes=[
            pltpu.VMEM(shape, block.dtype),
            pltpu.SemaphoreType.DMA((rows // 16,)),
        ],
        compiler_params=PARAMS,
        cost_estimate=COST,
    )(in_vmem(wide), in_vmem(block))


def add(left, right):
    return (left.astype(jnp.float32) + right.astype(jnp.float32)).astype(jnp.bfloat16)


def on_device(residual, queries, new_kv, cache_kv, lengths, out_weight):
    section_count = lax.axis_size("section")
    head_count = lax.axis_size("head")
    tick_count, row_count, head_width = queries.shape
    arrays = (queries, new_kv, cache_kv, out_weight)
    rows = row_count // head_count
    ticks = tuple(range(tick_count))

    def send(block, pairs, distance):
        route = [
            (s * head_count + a, (s + distance) % section_count * head_count + b)
            for s in range(section_count)
            for a, b in pairs
        ]
        return lax.ppermute(block, ("section", "head"), route)

    if head_count != 4 or tick_count != 2:
        partial, _ = first_rows(ticks, row_count, lambda z: 0, lambda z: z >= 0, lengths, *arrays)
        pieces = [
            lax.psum_scatter(block, "head", scatter_dimension=0, tiled=True) for block in partial
        ]
        updated = add(residual, jnp.stack(pieces, axis=1))
        return send(updated, [(i, i) for i in range(head_count)], 1)

    ends = [(0, 1), (3, 2)]
    middle = [(1, 2), (2, 1)]
    outward = [(0, 1), (3, 2), (1, 0), (2, 3)]

    def first(z):
        return jnp.where(z < 2, 3, 0)

    def second(z):
        return jnp.where(z < 2, 2, 1)

    def third(z):
        return jnp.where(z == 0, 1, jnp.where(z == 1, 0, jnp.where(z == 2, 3, 2)))

    def at_end(z):
        return (z == 0) | (z == head_count - 1)

    def in_middle(z):
        return jnp.logical_not(at_end(z))

    def third_or_second(z):
        return jnp.where(at_end(z), third(z), second(z))

    def everywhere(z):
        return z >= 0

    (a0_early,), loaded = first_rows((0,), rows, first, at_end, lengths, *arrays)
    a0_far = send(a0_early, ends, 0)
    (a0, a1), own_residual, held = second_rows(
        ticks, rows, first, at_end, lengths, arrays, residual, loaded, a0_early
    )
    a1_far = send(a1, ends, 0)
    (b,) = project_rows(ticks, rows, second, at_end, held, {}, COST, [a1])
    b_far = send(b, ends, 0)
    a0_sum = small_kernel(add_kernel, a0.shape, a0.dtype, COST, a0, a0_far, deps=[b])
    a0_mid = send(a0_sum, middle, 0)
    own = project_rows(
        ticks,
        rows,
        lambda z: z,
        everywhere,
        held,
        {"residual": own_residual},
        COST_OWN,
        [a0_sum],
        split=True,
    )
    own_here = [send(block, [(1, 1), (2, 2)], 1) for block in own]
    a1_sum = small_kernel(add_kernel, a1.shape, a1.dtype, COST_SUM, a1, a1_far, deps=[own[0]])
    a1_mid = send(a1_sum, middle, 0)
    (d,) = project_rows(
        ticks, rows, third_or_second, everywhere, held, {}, COST_D, [a1_sum, a0_mid]
    )
    (c,) = project_rows(ticks, rows, third, in_middle, held, {}, COST_C, [d])
    c_sum = small_kernel(
        functools.partial(outward_kernel, in_middle, tick_count),
        c.shape,
        c.dtype,
        COST,
        d,
        c,
        a0_mid,
        a1_mid,
        deps=own_here,
    )
    c_here = send(c_sum, outward, 1)
    d_sum = small_kernel(
        functools.partial(inner_kernel, in_middle, tick_count),
        d.shape,
        d.dtype,
        COST,
        *own,
        d,
        b_far,
        deps=[c_sum],
    )
    d_here = send(d_sum, middle + [(0, 0), (3, 3)], 1)
    wide = small_kernel(
        functools.partial(add_wide_kernel, tick_count),
        c.shape,
        jnp.float32,
        LONG,
        c_here,
        *own_here,
    )
    return finish(wide, d_here)


def solution(mesh):
    placed = (
        P(("section", "head"), None, None),
        P(None, "section", "head"),
        P(None, None, "section", None),
        P(None, "section", None),
        P(),
        P("section", "head", None),
    )
    return jax.shard_map(
        on_device,
        mesh=mesh,
        in_specs=placed,
        out_specs=P(("section", "head"), None, None),
        check_vma=False,
    )
```

```python
import functools
import math

import jax
import jax.numpy as jnp
from jax import lax
from jax.experimental import pallas as pl
from jax.experimental.pallas import tpu as pltpu
from jax.sharding import PartitionSpec as P

QH = 32
KVH = 8
HD = 128
GROUP = QH // KVH
KEY_BLOCK = 512
WEIGHT_PARTS = 4
COLUMN_TILE = 1024

neg_large = -1e30
EXPONENT = math.log2(math.e) / math.sqrt(HD)


def scores_of(query_rows, key_rows):
    return lax.dot_general(
        query_rows, key_rows, (((1,), (1,)), ((), ())), preferred_element_type=jnp.float32
    )


def attend(ticks, rows, row_first, my_length, query_of, fresh_ref, cache_ref, heads_ref):
    fresh_count = ticks[-1] + 1
    fresh_rows = fresh_ref.shape[2]
    capacity = cache_ref.shape[1]
    kv_count = fresh_ref.shape[3] // HD
    inner = heads_ref.shape[1] // HD // kv_count
    key_block = min(KEY_BLOCK, capacity)
    tick_rows = inner * rows
    all_rows = len(ticks) * tick_rows
    line = lax.broadcasted_iota(jnp.int32, (all_rows, fresh_rows), 0)
    position = lax.rem(line, rows) + row_first
    causal = lax.broadcasted_iota(jnp.int32, (all_rows, fresh_rows), 1) <= position
    for g in range(kv_count):
        lanes = slice(g * HD, (g + 1) * HD)
        query_rows = jnp.concatenate(
            [
                query_of(index, slice((g * inner + i) * HD, (g * inner + i + 1) * HD))
                for index in range(len(ticks))
                for i in range(inner)
            ],
            axis=0,
        )
        blocks = []
        for earlier in range(fresh_count):
            scores = scores_of(query_rows, fresh_ref[earlier, 0, :, lanes])
            if len(ticks) > 1:
                tick_here = line // tick_rows + ticks[0]
                seen = (tick_here > earlier) | ((tick_here == earlier) & causal)
                scores = jnp.where(seen, scores, neg_large)
            elif earlier == ticks[0]:
                scores = jnp.where(causal, scores, neg_large)
            blocks.append((scores, fresh_ref[earlier, 1, :, lanes]))
        for block in range(capacity // key_block):
            here = slice(block * key_block, (block + 1) * key_block)
            scores = scores_of(query_rows, cache_ref[0, here, lanes])
            column = lax.broadcasted_iota(jnp.int32, (1, key_block), 1)
            scores = scores + jnp.where(column < my_length - block * key_block, 0.0, neg_large)
            blocks.append((scores, cache_ref[1, here, lanes]))
        highest = None
        for scores, _ in blocks:
            for first in range(0, scores.shape[1], HD):
                part = scores[:, first : first + HD]
                highest = part if highest is None else jnp.maximum(highest, part)
        highest = jnp.max(highest, axis=1, keepdims=True)
        total = None
        for scores, values in blocks:
            weights = jnp.exp2((scores - highest) * EXPONENT).astype(jnp.bfloat16)
            wide = jnp.concatenate([values, jnp.ones_like(values)], axis=1)
            added = jnp.dot(weights, wide, preferred_element_type=jnp.float32)
            total = added if total is None else total + added
        mixed = (total[:, :HD] / total[:, HD:]).astype(jnp.bfloat16)
        for index in range(len(ticks)):
            for i in range(inner):
                head = g * inner + i
                first = (index * inner + i) * rows
                heads_ref[
                    index * rows : (index + 1) * rows, head * HD : (head + 1) * HD
                ] = mixed[first : first + rows]


def project(heads_ref, w_ref, outs):
    rows, columns = outs[0].shape
    tile = min(COLUMN_TILE, columns)
    for first in range(0, columns, tile):
        here = slice(first, first + tile)
        product = jnp.dot(heads_ref[...], w_ref[:, here], preferred_element_type=jnp.float32)
        for index, out in enumerate(outs):
            out[:, here] = product[index * rows : (index + 1) * rows].astype(out.dtype)


def project_arriving(heads_ref, w_ref, outs, sum_ref, copies):
    rows, columns = outs[0].shape
    tile = min(COLUMN_TILE, columns)
    part_rows = w_ref.shape[0] // len(copies)
    for part, copy in enumerate(copies):
        copy.wait()
        depth = slice(part * part_rows, (part + 1) * part_rows)
        for first in range(0, columns, tile):
            here = slice(first, first + tile)
            product = jnp.dot(
                heads_ref[:, depth], w_ref[depth, here], preferred_element_type=jnp.float32
            )
            if part > 0:
                product = product + sum_ref[:, here]
            if part < len(copies) - 1:
                sum_ref[:, here] = product
            else:
                for index, out in enumerate(outs):
                    out[:, here] = product[index * rows : (index + 1) * rows].astype(out.dtype)


def held_copies(new_kv, cache_kv, out_weight, fresh_ref, cache_ref, w_ref, sem):
    kv_width = cache_ref.shape[2]
    heads_here = w_ref.shape[0] // HD
    kv_column = pl.multiple_of(lax.axis_index("head") * heads_here // GROUP * HD, HD)
    lanes = pl.ds(kv_column, kv_width)
    pairs = []
    for tick in range(fresh_ref.shape[0]):
        for part in range(2):
            pairs.append((new_kv.at[tick, part, :, lanes], fresh_ref.at[tick, part]))
    for part in range(2):
        pairs.append((cache_kv.at[part, :, lanes], cache_ref.at[part]))
    part_rows = w_ref.shape[0] // WEIGHT_PARTS
    for part in range(WEIGHT_PARTS):
        here = pl.ds(part * part_rows, part_rows)
        pairs.append((out_weight.at[0, here, :], w_ref.at[here, :]))
    copies = [
        pltpu.make_async_copy(source, target, sem.at[index])
        for index, (source, target) in enumerate(pairs)
    ]
    return copies[:-WEIGHT_PARTS], copies[-WEIGHT_PARTS:]


def first_kernel(
    ticks, rows, choose, active, lengths, queries, new_kv, cache_kv, out_weight, *rest
):
    outs = rest[: len(ticks)]
    fresh_ref, cache_ref, w_ref, length_ref, q_ref, heads_ref, sum_ref, sem = rest[len(ticks) :]
    z = lax.axis_index("head")

    @pl.when(active(z))
    def _():
        row_first = pl.multiple_of(choose(z) * rows, rows)
        copies, w_copies = held_copies(
            new_kv, cache_kv, out_weight, fresh_ref, cache_ref, w_ref, sem
        )
        used = len(copies) + len(w_copies)
        copies.append(pltpu.make_async_copy(lengths, length_ref, sem.at[used]))
        for index, tick in enumerate(ticks):
            copies.append(
                pltpu.make_async_copy(
                    queries.at[tick, pl.ds(row_first, rows), :],
                    q_ref.at[index],
                    sem.at[used + 1 + index],
                )
            )
        early = len(w_copies) // 2
        for copy in copies + w_copies[:early]:
            copy.start()
        for copy in copies:
            copy.wait()
        for copy in w_copies[early:]:
            copy.start()
        attend(
            ticks,
            rows,
            row_first,
            length_ref[lax.axis_index("section")],
            lambda index, lanes: q_ref[index, :, lanes],
            fresh_ref,
            cache_ref,
            heads_ref,
        )
        project_arriving(heads_ref, w_ref, outs, sum_ref, w_copies)


def later_rows(ticks, rows, choose, lengths, q_ref, fresh_ref, cache_ref, heads_ref):
    row_first = pl.multiple_of(choose(lax.axis_index("head")) * rows, rows)
    attend(
        ticks,
        rows,
        row_first,
        lengths[lax.axis_index("section")],
        lambda index, lanes: q_ref[ticks[index], pl.ds(row_first, rows), lanes],
        fresh_ref,
        cache_ref,
        heads_ref,
    )


def second_kernel(
    ticks,
    rows,
    choose,
    active,
    lengths,
    queries,
    new_kv,
    cache_kv,
    out_weight,
    residual,
    fresh_in,
    cache_in,
    w_in,
    dep,
    *rest,
):
    outs = rest[: len(ticks)]
    q_ref, by_tick_ref, fresh_ref, cache_ref, w_ref, *scratch = rest[len(ticks) :]
    heads_ref, residual_ref, sem, q_sem, residual_sem = scratch
    late = jnp.logical_not(active(lax.axis_index("head")))
    copies, w_copies = held_copies(new_kv, cache_kv, out_weight, fresh_ref, cache_ref, w_ref, sem)
    q_copy = pltpu.make_async_copy(queries, q_ref, q_sem)
    q_copy.start()
    residual_copy = pltpu.make_async_copy(residual, residual_ref, residual_sem)
    residual_copy.start()

    @pl.when(late)
    def _():
        for copy in copies + w_copies:
            copy.start()
        for copy in copies:
            copy.wait()

    q_copy.wait()
    later_rows(ticks, rows, choose, lengths, q_ref, fresh_ref, cache_ref, heads_ref)

    @pl.when(late)
    def _():
        for copy in w_copies:
            copy.wait()

    project(heads_ref, w_ref, outs)
    residual_copy.wait()
    for tick in range(by_tick_ref.shape[0]):
        by_tick_ref[tick] = residual_ref[:, tick, :]


def plus(left, right, out):
    out[...] = (left[...].astype(jnp.float32) + right[...].astype(jnp.float32)).astype(out.dtype)


def rows_kernel(ticks, rows, choose, names, *refs):
    ref = dict(zip(names, refs))
    if "out" in ref:
        outs = [ref["out"].at[index] for index in range(len(ticks))]
    else:
        outs = [ref["out%d" % tick] for tick in ticks]
    later_rows(
        ticks, rows, choose, ref["lengths"], ref["q"], ref["fresh"], ref["cache"], ref["heads"]
    )
    project(ref["heads"], ref["w"], outs)
    if "residual" in ref:
        for index, out in enumerate(outs):
            plus(out, ref["residual"].at[index], out)


def in_vmem(array):
    return pltpu.with_memory_space_constraint(array, pltpu.VMEM)


def in_hbm(array):
    return pltpu.with_memory_space_constraint(array, pltpu.HBM)


WHOLE = pl.BlockSpec(memory_space=pltpu.VMEM)
ANYWHERE = pl.BlockSpec(memory_space=pl.ANY)
PARAMS = pltpu.CompilerParams(vmem_limit_bytes=28 * 2**20)
def cost_of(flops):
    return pl.CostEstimate(flops=flops, bytes_accessed=1000, transcendentals=0)


COST = cost_of(1000)
COST_X = cost_of(1000)
COST_Y = cost_of(4500000000)
COST_SUM = cost_of(1000)
COST_V = cost_of(1000)
COST_CS = cost_of(1000)
COST_W = cost_of(1000)
COST_D = [cost_of(4500000000), cost_of(1000)]


def held_shapes(queries, new_kv, cache_kv, out_weight):
    tick_count, row_count, head_width = queries.shape
    kv_width = max(1, head_width // HD // GROUP) * HD
    kind = queries.dtype
    return [
        pltpu.VMEM((tick_count, 2, row_count, kv_width), kind),
        pltpu.VMEM((2, cache_kv.shape[1], kv_width), kind),
        pltpu.VMEM((head_width, out_weight.shape[2]), kind),
    ]


def first_rows(ticks, rows, choose, active, lengths, *arrays):
    queries, out_weight = arrays[0], arrays[3]
    tick_count, row_count, head_width = queries.shape
    columns = out_weight.shape[2]
    kind = queries.dtype
    out_shape = [pltpu.VMEM((rows, columns), kind)] * len(ticks) + held_shapes(*arrays)
    results = pl.pallas_call(
        functools.partial(first_kernel, ticks, rows, choose, active),
        out_shape=out_shape,
        in_specs=[ANYWHERE] * 5,
        out_specs=[WHOLE] * len(out_shape),
        scratch_shapes=[
            pltpu.SMEM(lengths.shape, lengths.dtype),
            pltpu.VMEM((len(ticks), rows, head_width), kind),
            pltpu.VMEM((len(ticks) * rows, head_width), kind),
            pltpu.VMEM((len(ticks) * rows, columns), jnp.float32),
            pltpu.SemaphoreType.DMA((3 + 2 * tick_count + WEIGHT_PARTS + len(ticks),)),
        ],
        compiler_params=PARAMS,
        cost_estimate=COST,
    )(*[in_hbm(array) for array in (lengths, *arrays)])
    return results[: len(ticks)], results[len(ticks) :]


def second_rows(ticks, rows, choose, active, lengths, arrays, residual, held, dep):
    queries, out_weight = arrays[0], arrays[3]
    tick_count, row_count, head_width = queries.shape
    kind = queries.dtype
    out_shape = [pltpu.VMEM((rows, out_weight.shape[2]), kind)] * len(ticks)
    out_shape += [
        pltpu.VMEM(queries.shape, kind),
        pltpu.VMEM((tick_count, residual.shape[0], residual.shape[2]), kind),
    ] + held_shapes(*arrays)
    results = pl.pallas_call(
        functools.partial(second_kernel, ticks, rows, choose, active),
        out_shape=out_shape,
        in_specs=[pl.BlockSpec(memory_space=pltpu.SMEM)] + [ANYWHERE] * 5 + [WHOLE] * 3 + [ANYWHERE],
        out_specs=[WHOLE] * len(out_shape),
        scratch_shapes=[
            pltpu.VMEM((len(ticks) * rows, head_width), kind),
            pltpu.VMEM(residual.shape, kind),
            pltpu.SemaphoreType.DMA((2 + 2 * tick_count + WEIGHT_PARTS,)),
            pltpu.SemaphoreType.DMA,
            pltpu.SemaphoreType.DMA,
        ],
        input_output_aliases={6 + index: len(ticks) + 2 + index for index in range(3)},
        compiler_params=PARAMS,
        cost_estimate=COST,
    )(
        lengths,
        *[in_hbm(array) for array in (*arrays, residual)],
        *[in_vmem(array) for array in held],
        dep,
    )
    here = len(ticks)
    return results[:here], results[here + 1], (lengths, results[here], *results[here + 2 :])


def project_rows(ticks, rows, choose, held, cost, deps, residual=None, split=True):
    lengths, queries, fresh, cache, weight = held
    columns = weight.shape[1]
    kind = queries.dtype
    operands = {"q": queries, "fresh": fresh, "cache": cache, "w": weight}
    if residual is not None:
        operands["residual"] = residual
    names = ["lengths"] + list(operands) + ["dep"] * len(deps)
    if split:
        outs = {"out%d" % tick: pltpu.VMEM((rows, columns), kind) for tick in ticks}
    else:
        outs = {"out": pltpu.VMEM((len(ticks), rows, columns), kind)}
    names += list(outs) + ["heads"]
    return pl.pallas_call(
        functools.partial(rows_kernel, ticks, rows, choose, names),
        out_shape=list(outs.values()),
        in_specs=[pl.BlockSpec(memory_space=pltpu.SMEM)]
        + [WHOLE] * len(operands)
        + [ANYWHERE] * len(deps),
        out_specs=[WHOLE] * len(outs),
        scratch_shapes=[pltpu.VMEM((len(ticks) * rows, queries.shape[2]), kind)],
        compiler_params=PARAMS,
        cost_estimate=cost,
    )(lengths, *[in_vmem(array) for array in operands.values()], *deps)


def small_kernel(kernel, shape, kind, cost, *blocks, deps=()):
    return pl.pallas_call(
        kernel,
        out_shape=pltpu.VMEM(shape, kind),
        in_specs=[WHOLE] * len(blocks) + [ANYWHERE] * len(deps),
        out_specs=WHOLE,
        compiler_params=PARAMS,
        cost_estimate=cost,
    )(*blocks, *deps)


def add_kernel(left, right, *rest):
    plus(left, right, rest[-1])


def by_role_kernel(active, count, *refs):
    out = refs[-1]
    plain, left, right = refs[:count], refs[count : 2 * count], refs[2 * count : 3 * count]
    here = active(lax.axis_index("head"))

    @pl.when(here)
    def _():
        for index in range(count):
            plus(left[index], right[index], out.at[index])

    @pl.when(jnp.logical_not(here))
    def _():
        for index in range(count):
            out[index] = plain[index][...]


def inner_kernel(active, tick, plain, left, right, *rest):
    out = rest[-1]
    here = active(lax.axis_index("head"))

    @pl.when(here)
    def _():
        plus(left, right, out)

    @pl.when(jnp.logical_not(here))
    def _():
        out[...] = plain[tick]


def wide_kernel(block, *refs):
    out = refs[-1]
    for tick in range(out.shape[0]):
        out[tick] = block[tick].astype(jnp.float32) + refs[tick][...].astype(jnp.float32)


def finish_kernel(wide, block, out, buf, sem):
    step = 16
    copies = []
    for first in range(0, out.shape[0], step):
        here = pl.ds(first, step)
        for tick in range(out.shape[1]):
            total = wide[tick, here, :] + block[tick, here, :].astype(jnp.float32)
            buf[here, tick, :] = total.astype(out.dtype)
        copies.append(pltpu.make_async_copy(buf.at[here], out.at[here], sem.at[first // step]))
        copies[-1].start()
    for copy in copies:
        copy.wait()


def finish(wide, block):
    tick_count, rows, columns = wide.shape
    shape = (rows, tick_count, columns)
    return pl.pallas_call(
        finish_kernel,
        out_shape=jax.ShapeDtypeStruct(shape, block.dtype),
        in_specs=[WHOLE] * 2,
        out_specs=ANYWHERE,
        scratch_shapes=[
            pltpu.VMEM(shape, block.dtype),
            pltpu.SemaphoreType.DMA((rows // 16,)),
        ],
        compiler_params=PARAMS,
        cost_estimate=COST,
    )(in_vmem(wide), in_vmem(block))


def add(left, right):
    return (left.astype(jnp.float32) + right.astype(jnp.float32)).astype(jnp.bfloat16)


def on_device(residual, queries, new_kv, cache_kv, lengths, out_weight):
    section_count = lax.axis_size("section")
    head_count = lax.axis_size("head")
    tick_count, row_count, head_width = queries.shape
    arrays = (queries, new_kv, cache_kv, out_weight)
    rows = row_count // head_count
    ticks = tuple(range(tick_count))

    def send(block, pairs, distance):
        route = [
            (s * head_count + a, (s + distance) % section_count * head_count + b)
            for s in range(section_count)
            for a, b in pairs
        ]
        return lax.ppermute(block, ("section", "head"), route)

    if head_count != 4 or tick_count != 2:
        partial, _ = first_rows(ticks, row_count, lambda z: 0, lambda z: z >= 0, lengths, *arrays)
        pieces = [
            lax.psum_scatter(block, "head", scatter_dimension=0, tiled=True) for block in partial
        ]
        updated = add(residual, jnp.stack(pieces, axis=1))
        return send(updated, [(i, i) for i in range(head_count)], 1)

    ends = [(0, 1), (3, 2)]
    middle = [(1, 2), (2, 1)]
    outward = [(0, 1), (3, 2), (1, 0), (2, 3)]

    def first(z):
        return jnp.where(z < 2, 3, 0)

    def second(z):
        return jnp.where(z < 2, 2, 1)

    def third(z):
        return jnp.where(z == 0, 1, jnp.where(z == 1, 0, jnp.where(z == 2, 3, 2)))

    def at_end(z):
        return (z == 0) | (z == head_count - 1)

    def in_middle(z):
        return jnp.logical_not(at_end(z))

    def by_role(at_ends, in_the_middle):
        return lambda z: jnp.where(at_end(z), at_ends(z), in_the_middle(z))

    (a0_early,), loaded = first_rows((0,), rows, first, at_end, lengths, *arrays)
    a0_far = send(a0_early, ends, 0)
    (a0, a1), own_residual, held = second_rows(
        ticks, rows, first, at_end, lengths, arrays, residual, loaded, a0_early
    )
    a1_far = send(a1, ends, 0)
    x = project_rows(ticks, rows, by_role(second, third), held, COST_X, [a1])
    x_far = [send(block, ends, 0) for block in x]
    a0_sum = small_kernel(add_kernel, a0.shape, a0.dtype, COST, a0, a0_far, deps=[x[0]])
    a0_mid = send(a0_sum, middle, 0)
    (y,) = project_rows(
        ticks, rows, lambda z: z, held, COST_Y, [a0_sum], own_residual, split=False
    )
    y_here = send(y, [(1, 1), (2, 2)], 1)
    a1_sum = small_kernel(add_kernel, a1.shape, a1.dtype, COST_SUM, a1, a1_far, deps=[y])
    a1_mid = send(a1_sum, middle, 0)
    v = project_rows(
        ticks, rows, by_role(third, second), held, COST_V, [a1_sum, a0_mid, x_far[0]]
    )
    both = (tick_count,) + a0.shape
    c_sum = small_kernel(
        functools.partial(by_role_kernel, in_middle, tick_count),
        both,
        a0.dtype,
        COST_CS,
        *v,
        *x,
        a0_mid,
        a1_mid,
    )
    c_here = send(c_sum, outward, 1)
    d_here = []
    deps = [c_sum]
    for tick in ticks:
        d_sum = small_kernel(
            functools.partial(inner_kernel, in_middle, tick),
            a0.shape,
            a0.dtype,
            COST_D[tick],
            y,
            v[tick],
            x_far[tick],
            deps=deps,
        )
        d_here.append(send(d_sum, middle + [(0, 0), (3, 3)], 1))
        deps = [c_sum, y_here]
    wide = small_kernel(wide_kernel, both, jnp.float32, COST_W, y_here, *d_here)
    return finish(wide, c_here)


def solution(mesh):
    placed = (
        P(("section", "head"), None, None),
        P(None, "section", "head"),
        P(None, None, "section", None),
        P(None, "section", None),
        P(),
        P("section", "head", None),
    )
    return jax.shard_map(
        on_device,
        mesh=mesh,
        in_specs=placed,
        out_specs=P(("section", "head"), None, None),
        check_vma=False,
    )
```

```python
import functools
import math

import jax
import jax.numpy as jnp
from jax import lax
from jax.experimental import pallas as pl
from jax.experimental.pallas import tpu as pltpu
from jax.sharding import PartitionSpec as P

QH = 32
KVH = 8
HD = 128
GROUP = QH // KVH
KEY_BLOCK = 512
WEIGHT_PARTS = 2
COLUMN_TILE = 1024

neg_large = -1e30
EXPONENT = math.log2(math.e) / math.sqrt(HD)


def scores_of(query_rows, key_rows):
    return lax.dot_general(
        query_rows, key_rows, (((1,), (1,)), ((), ())), preferred_element_type=jnp.float32
    )


def attend(ticks, rows, row_first, my_length, query_of, fresh_ref, cache_ref, heads_ref):
    fresh_count = ticks[-1] + 1
    fresh_rows = fresh_ref.shape[2]
    capacity = cache_ref.shape[1]
    kv_count = fresh_ref.shape[3] // HD
    inner = heads_ref.shape[1] // HD // kv_count
    key_block = min(KEY_BLOCK, capacity)
    tick_rows = inner * rows
    all_rows = len(ticks) * tick_rows
    line = lax.broadcasted_iota(jnp.int32, (all_rows, fresh_rows), 0)
    position = lax.rem(line, rows) + row_first
    causal = lax.broadcasted_iota(jnp.int32, (all_rows, fresh_rows), 1) <= position
    for g in range(kv_count):
        lanes = slice(g * HD, (g + 1) * HD)
        query_rows = jnp.concatenate(
            [
                query_of(index, slice((g * inner + i) * HD, (g * inner + i + 1) * HD))
                for index in range(len(ticks))
                for i in range(inner)
            ],
            axis=0,
        )
        blocks = []
        for earlier in range(fresh_count):
            scores = scores_of(query_rows, fresh_ref[earlier, 0, :, lanes])
            if len(ticks) > 1:
                tick_here = line // tick_rows + ticks[0]
                seen = (tick_here > earlier) | ((tick_here == earlier) & causal)
                scores = jnp.where(seen, scores, neg_large)
            elif earlier == ticks[0]:
                scores = jnp.where(causal, scores, neg_large)
            blocks.append((scores, fresh_ref[earlier, 1, :, lanes]))
        for block in range(capacity // key_block):
            here = slice(block * key_block, (block + 1) * key_block)
            scores = scores_of(query_rows, cache_ref[0, here, lanes])
            column = lax.broadcasted_iota(jnp.int32, (1, key_block), 1)
            scores = scores + jnp.where(column < my_length - block * key_block, 0.0, neg_large)
            blocks.append((scores, cache_ref[1, here, lanes]))
        highest = None
        for scores, _ in blocks:
            for first in range(0, scores.shape[1], HD):
                part = scores[:, first : first + HD]
                highest = part if highest is None else jnp.maximum(highest, part)
        highest = jnp.max(highest, axis=1, keepdims=True)
        total = None
        for scores, values in blocks:
            weights = jnp.exp2((scores - highest) * EXPONENT).astype(jnp.bfloat16)
            wide = jnp.concatenate([values, jnp.ones_like(values)], axis=1)
            added = jnp.dot(weights, wide, preferred_element_type=jnp.float32)
            total = added if total is None else total + added
        mixed = (total[:, :HD] / total[:, HD:]).astype(jnp.bfloat16)
        for index in range(len(ticks)):
            for i in range(inner):
                head = g * inner + i
                first = (index * inner + i) * rows
                heads_ref[
                    index * rows : (index + 1) * rows, head * HD : (head + 1) * HD
                ] = mixed[first : first + rows]


def project(heads_ref, w_ref, outs):
    rows, columns = outs[0].shape
    tile = min(COLUMN_TILE, columns)
    for first in range(0, columns, tile):
        here = slice(first, first + tile)
        product = jnp.dot(heads_ref[...], w_ref[:, here], preferred_element_type=jnp.float32)
        for index, out in enumerate(outs):
            out[:, here] = product[index * rows : (index + 1) * rows].astype(out.dtype)


def project_arriving(heads_ref, w_ref, outs, sum_ref, copies):
    rows, columns = outs[0].shape
    tile = min(COLUMN_TILE, columns)
    part_rows = w_ref.shape[0] // len(copies)
    for part, copy in enumerate(copies):
        copy.wait()
        depth = slice(part * part_rows, (part + 1) * part_rows)
        for first in range(0, columns, tile):
            here = slice(first, first + tile)
            product = jnp.dot(
                heads_ref[:, depth], w_ref[depth, here], preferred_element_type=jnp.float32
            )
            if part > 0:
                product = product + sum_ref[:, here]
            if part < len(copies) - 1:
                sum_ref[:, here] = product
            else:
                for index, out in enumerate(outs):
                    out[:, here] = product[index * rows : (index + 1) * rows].astype(out.dtype)


def held_copies(new_kv, cache_kv, out_weight, fresh_ref, cache_ref, w_ref, sem):
    kv_width = cache_ref.shape[2]
    heads_here = w_ref.shape[0] // HD
    kv_column = pl.multiple_of(lax.axis_index("head") * heads_here // GROUP * HD, HD)
    lanes = pl.ds(kv_column, kv_width)
    pairs = []
    for tick in range(fresh_ref.shape[0]):
        for part in range(2):
            pairs.append((new_kv.at[tick, part, :, lanes], fresh_ref.at[tick, part]))
    for part in range(2):
        pairs.append((cache_kv.at[part, :, lanes], cache_ref.at[part]))
    part_rows = w_ref.shape[0] // WEIGHT_PARTS
    for part in range(WEIGHT_PARTS):
        here = pl.ds(part * part_rows, part_rows)
        pairs.append((out_weight.at[0, here, :], w_ref.at[here, :]))
    copies = [
        pltpu.make_async_copy(source, target, sem.at[index])
        for index, (source, target) in enumerate(pairs)
    ]
    return copies[:-WEIGHT_PARTS], copies[-WEIGHT_PARTS:]


def first_kernel(
    ticks, rows, choose, active, lengths, queries, new_kv, cache_kv, out_weight, *rest
):
    outs = rest[: len(ticks)]
    fresh_ref, cache_ref, w_ref, length_ref, q_ref, heads_ref, sum_ref, sem = rest[len(ticks) :]
    z = lax.axis_index("head")

    @pl.when(active(z))
    def _():
        row_first = pl.multiple_of(choose(z) * rows, rows)
        copies, w_copies = held_copies(
            new_kv, cache_kv, out_weight, fresh_ref, cache_ref, w_ref, sem
        )
        used = len(copies) + len(w_copies)
        copies.append(pltpu.make_async_copy(lengths, length_ref, sem.at[used]))
        for index, tick in enumerate(ticks):
            copies.append(
                pltpu.make_async_copy(
                    queries.at[tick, pl.ds(row_first, rows), :],
                    q_ref.at[index],
                    sem.at[used + 1 + index],
                )
            )
        early = len(w_copies)
        for copy in copies + w_copies[:early]:
            copy.start()
        for copy in copies:
            copy.wait()
        for copy in w_copies[early:]:
            copy.start()
        attend(
            ticks,
            rows,
            row_first,
            length_ref[lax.axis_index("section")],
            lambda index, lanes: q_ref[index, :, lanes],
            fresh_ref,
            cache_ref,
            heads_ref,
        )
        project_arriving(heads_ref, w_ref, outs, sum_ref, w_copies)


def later_rows(ticks, rows, choose, lengths, q_ref, fresh_ref, cache_ref, heads_ref):
    row_first = pl.multiple_of(choose(lax.axis_index("head")) * rows, rows)
    attend(
        ticks,
        rows,
        row_first,
        lengths[lax.axis_index("section")],
        lambda index, lanes: q_ref[ticks[index], pl.ds(row_first, rows), lanes],
        fresh_ref,
        cache_ref,
        heads_ref,
    )


def second_kernel(
    ticks,
    rows,
    choose,
    active,
    lengths,
    queries,
    new_kv,
    cache_kv,
    out_weight,
    residual,
    fresh_in,
    cache_in,
    w_in,
    dep,
    *rest,
):
    outs = rest[: len(ticks)]
    q_ref, by_tick_ref, fresh_ref, cache_ref, w_ref, *scratch = rest[len(ticks) :]
    heads_ref, residual_ref, sem, q_sem, residual_sem = scratch
    late = jnp.logical_not(active(lax.axis_index("head")))
    copies, w_copies = held_copies(new_kv, cache_kv, out_weight, fresh_ref, cache_ref, w_ref, sem)
    q_copy = pltpu.make_async_copy(queries, q_ref, q_sem)
    q_copy.start()
    residual_copy = pltpu.make_async_copy(residual, residual_ref, residual_sem)
    residual_copy.start()

    @pl.when(late)
    def _():
        for copy in copies + w_copies:
            copy.start()
        for copy in copies:
            copy.wait()

    q_copy.wait()
    later_rows(ticks, rows, choose, lengths, q_ref, fresh_ref, cache_ref, heads_ref)

    @pl.when(late)
    def _():
        for copy in w_copies:
            copy.wait()

    project(heads_ref, w_ref, outs)
    residual_copy.wait()
    for tick in range(by_tick_ref.shape[0]):
        by_tick_ref[tick] = residual_ref[:, tick, :]


def plus(left, right, out):
    out[...] = (left[...].astype(jnp.float32) + right[...].astype(jnp.float32)).astype(out.dtype)


def rows_kernel(ticks, rows, choose, names, *refs):
    ref = dict(zip(names, refs))
    if "out" in ref:
        outs = [ref["out"].at[index] for index in range(len(ticks))]
    else:
        outs = [ref["out%d" % tick] for tick in ticks]
    later_rows(
        ticks, rows, choose, ref["lengths"], ref["q"], ref["fresh"], ref["cache"], ref["heads"]
    )
    project(ref["heads"], ref["w"], outs)
    if "residual" in ref:
        for index, out in enumerate(outs):
            plus(out, ref["residual"].at[index], out)


def in_vmem(array):
    return pltpu.with_memory_space_constraint(array, pltpu.VMEM)


def in_hbm(array):
    return pltpu.with_memory_space_constraint(array, pltpu.HBM)


WHOLE = pl.BlockSpec(memory_space=pltpu.VMEM)
ANYWHERE = pl.BlockSpec(memory_space=pl.ANY)
PARAMS = pltpu.CompilerParams(vmem_limit_bytes=28 * 2**20)
def cost_of(flops):
    return pl.CostEstimate(flops=flops, bytes_accessed=1000, transcendentals=0)


COST = cost_of(1000)
COST_X = cost_of(1000)
COST_Y = cost_of(4500000000)
COST_SUM = cost_of(1000)
COST_V = cost_of(1000)
COST_CS = cost_of(1000)
COST_W = cost_of(1000)
COST_D = [cost_of(4500000000), cost_of(1000)]


def held_shapes(queries, new_kv, cache_kv, out_weight):
    tick_count, row_count, head_width = queries.shape
    kv_width = max(1, head_width // HD // GROUP) * HD
    kind = queries.dtype
    return [
        pltpu.VMEM((tick_count, 2, row_count, kv_width), kind),
        pltpu.VMEM((2, cache_kv.shape[1], kv_width), kind),
        pltpu.VMEM((head_width, out_weight.shape[2]), kind),
    ]


def first_rows(ticks, rows, choose, active, lengths, *arrays):
    queries, out_weight = arrays[0], arrays[3]
    tick_count, row_count, head_width = queries.shape
    columns = out_weight.shape[2]
    kind = queries.dtype
    out_shape = [pltpu.VMEM((rows, columns), kind)] * len(ticks) + held_shapes(*arrays)
    results = pl.pallas_call(
        functools.partial(first_kernel, ticks, rows, choose, active),
        out_shape=out_shape,
        in_specs=[ANYWHERE] * 5,
        out_specs=[WHOLE] * len(out_shape),
        scratch_shapes=[
            pltpu.SMEM(lengths.shape, lengths.dtype),
            pltpu.VMEM((len(ticks), rows, head_width), kind),
            pltpu.VMEM((len(ticks) * rows, head_width), kind),
            pltpu.VMEM((len(ticks) * rows, columns), jnp.float32),
            pltpu.SemaphoreType.DMA((3 + 2 * tick_count + WEIGHT_PARTS + len(ticks),)),
        ],
        compiler_params=PARAMS,
        cost_estimate=COST,
    )(*[in_hbm(array) for array in (lengths, *arrays)])
    return results[: len(ticks)], results[len(ticks) :]


def second_rows(ticks, rows, choose, active, lengths, arrays, residual, held, dep):
    queries, out_weight = arrays[0], arrays[3]
    tick_count, row_count, head_width = queries.shape
    kind = queries.dtype
    out_shape = [pltpu.VMEM((rows, out_weight.shape[2]), kind)] * len(ticks)
    out_shape += [
        pltpu.VMEM(queries.shape, kind),
        pltpu.VMEM((tick_count, residual.shape[0], residual.shape[2]), kind),
    ] + held_shapes(*arrays)
    results = pl.pallas_call(
        functools.partial(second_kernel, ticks, rows, choose, active),
        out_shape=out_shape,
        in_specs=[pl.BlockSpec(memory_space=pltpu.SMEM)] + [ANYWHERE] * 5 + [WHOLE] * 3 + [ANYWHERE],
        out_specs=[WHOLE] * len(out_shape),
        scratch_shapes=[
            pltpu.VMEM((len(ticks) * rows, head_width), kind),
            pltpu.VMEM(residual.shape, kind),
            pltpu.SemaphoreType.DMA((2 + 2 * tick_count + WEIGHT_PARTS,)),
            pltpu.SemaphoreType.DMA,
            pltpu.SemaphoreType.DMA,
        ],
        input_output_aliases={6 + index: len(ticks) + 2 + index for index in range(3)},
        compiler_params=PARAMS,
        cost_estimate=COST,
    )(
        lengths,
        *[in_hbm(array) for array in (*arrays, residual)],
        *[in_vmem(array) for array in held],
        dep,
    )
    here = len(ticks)
    return results[:here], results[here + 1], (lengths, results[here], *results[here + 2 :])


def project_rows(ticks, rows, choose, held, cost, deps, residual=None, split=True):
    lengths, queries, fresh, cache, weight = held
    columns = weight.shape[1]
    kind = queries.dtype
    operands = {"q": queries, "fresh": fresh, "cache": cache, "w": weight}
    if residual is not None:
        operands["residual"] = residual
    names = ["lengths"] + list(operands) + ["dep"] * len(deps)
    if split:
        outs = {"out%d" % tick: pltpu.VMEM((rows, columns), kind) for tick in ticks}
    else:
        outs = {"out": pltpu.VMEM((len(ticks), rows, columns), kind)}
    names += list(outs) + ["heads"]
    return pl.pallas_call(
        functools.partial(rows_kernel, ticks, rows, choose, names),
        out_shape=list(outs.values()),
        in_specs=[pl.BlockSpec(memory_space=pltpu.SMEM)]
        + [WHOLE] * len(operands)
        + [ANYWHERE] * len(deps),
        out_specs=[WHOLE] * len(outs),
        scratch_shapes=[pltpu.VMEM((len(ticks) * rows, queries.shape[2]), kind)],
        compiler_params=PARAMS,
        cost_estimate=cost,
    )(lengths, *[in_vmem(array) for array in operands.values()], *deps)


def small_kernel(kernel, shape, kind, cost, *blocks, deps=()):
    return pl.pallas_call(
        kernel,
        out_shape=pltpu.VMEM(shape, kind),
        in_specs=[WHOLE] * len(blocks) + [ANYWHERE] * len(deps),
        out_specs=WHOLE,
        compiler_params=PARAMS,
        cost_estimate=cost,
    )(*blocks, *deps)


def add_kernel(left, right, *rest):
    plus(left, right, rest[-1])


def by_role_kernel(active, count, *refs):
    out = refs[-1]
    plain, left, right = refs[:count], refs[count : 2 * count], refs[2 * count : 3 * count]
    here = active(lax.axis_index("head"))

    @pl.when(here)
    def _():
        for index in range(count):
            plus(left[index], right[index], out.at[index])

    @pl.when(jnp.logical_not(here))
    def _():
        for index in range(count):
            out[index] = plain[index][...]


def inner_kernel(active, tick, plain, left, right, *rest):
    out = rest[-1]
    here = active(lax.axis_index("head"))

    @pl.when(here)
    def _():
        plus(left, right, out)

    @pl.when(jnp.logical_not(here))
    def _():
        out[...] = plain[tick]


def wide_kernel(block, *refs):
    out = refs[-1]
    for tick in range(out.shape[0]):
        out[tick] = block[tick].astype(jnp.float32) + refs[tick][...].astype(jnp.float32)


def finish_kernel(wide, block, out, buf, sem):
    step = 16
    copies = []
    for first in range(0, out.shape[0], step):
        here = pl.ds(first, step)
        for tick in range(out.shape[1]):
            total = wide[tick, here, :] + block[tick, here, :].astype(jnp.float32)
            buf[here, tick, :] = total.astype(out.dtype)
        copies.append(pltpu.make_async_copy(buf.at[here], out.at[here], sem.at[first // step]))
        copies[-1].start()
    for copy in copies:
        copy.wait()


def finish(wide, block):
    tick_count, rows, columns = wide.shape
    shape = (rows, tick_count, columns)
    return pl.pallas_call(
        finish_kernel,
        out_shape=jax.ShapeDtypeStruct(shape, block.dtype),
        in_specs=[WHOLE] * 2,
        out_specs=ANYWHERE,
        scratch_shapes=[
            pltpu.VMEM(shape, block.dtype),
            pltpu.SemaphoreType.DMA((rows // 16,)),
        ],
        compiler_params=PARAMS,
        cost_estimate=COST,
    )(in_vmem(wide), in_vmem(block))


def add(left, right):
    return (left.astype(jnp.float32) + right.astype(jnp.float32)).astype(jnp.bfloat16)


def on_device(residual, queries, new_kv, cache_kv, lengths, out_weight):
    section_count = lax.axis_size("section")
    head_count = lax.axis_size("head")
    tick_count, row_count, head_width = queries.shape
    arrays = (queries, new_kv, cache_kv, out_weight)
    rows = row_count // head_count
    ticks = tuple(range(tick_count))

    def send(block, pairs, distance):
        route = [
            (s * head_count + a, (s + distance) % section_count * head_count + b)
            for s in range(section_count)
            for a, b in pairs
        ]
        return lax.ppermute(block, ("section", "head"), route)

    if head_count != 4 or tick_count != 2:
        partial, _ = first_rows(ticks, row_count, lambda z: 0, lambda z: z >= 0, lengths, *arrays)
        pieces = [
            lax.psum_scatter(block, "head", scatter_dimension=0, tiled=True) for block in partial
        ]
        updated = add(residual, jnp.stack(pieces, axis=1))
        return send(updated, [(i, i) for i in range(head_count)], 1)

    ends = [(0, 1), (3, 2)]
    middle = [(1, 2), (2, 1)]
    outward = [(0, 1), (3, 2), (1, 0), (2, 3)]

    def first(z):
        return jnp.where(z < 2, 3, 0)

    def second(z):
        return jnp.where(z < 2, 2, 1)

    def third(z):
        return jnp.where(z == 0, 1, jnp.where(z == 1, 0, jnp.where(z == 2, 3, 2)))

    def at_end(z):
        return (z == 0) | (z == head_count - 1)

    def in_middle(z):
        return jnp.logical_not(at_end(z))

    def by_role(at_ends, in_the_middle):
        return lambda z: jnp.where(at_end(z), at_ends(z), in_the_middle(z))

    (a0_early,), loaded = first_rows((0,), rows, first, at_end, lengths, *arrays)
    a0_far = send(a0_early, ends, 0)
    (a0, a1), own_residual, held = second_rows(
        ticks, rows, first, at_end, lengths, arrays, residual, loaded, a0_early
    )
    a1_far = send(a1, ends, 0)
    x = project_rows(ticks, rows, by_role(second, third), held, COST_X, [a1])
    x_far = [send(block, ends, 0) for block in x]
    a0_sum = small_kernel(add_kernel, a0.shape, a0.dtype, COST, a0, a0_far, deps=[x[0]])
    a0_mid = send(a0_sum, middle, 0)
    (y,) = project_rows(
        ticks, rows, lambda z: z, held, COST_Y, [a0_sum], own_residual, split=False
    )
    y_here = send(y, [(1, 1), (2, 2)], 1)
    a1_sum = small_kernel(add_kernel, a1.shape, a1.dtype, COST_SUM, a1, a1_far, deps=[y])
    a1_mid = send(a1_sum, middle, 0)
    v = project_rows(
        ticks, rows, by_role(third, second), held, COST_V, [a1_sum, a0_mid, x_far[0]]
    )
    both = (tick_count,) + a0.shape
    c_sum = small_kernel(
        functools.partial(by_role_kernel, in_middle, tick_count),
        both,
        a0.dtype,
        COST_CS,
        *v,
        *x,
        a0_mid,
        a1_mid,
    )
    c_here = send(c_sum, outward, 1)
    d_here = []
    deps = [c_sum]
    for tick in ticks:
        d_sum = small_kernel(
            functools.partial(inner_kernel, in_middle, tick),
            a0.shape,
            a0.dtype,
            COST_D[tick],
            y,
            v[tick],
            x_far[tick],
            deps=deps,
        )
        d_here.append(send(d_sum, middle + [(0, 0), (3, 3)], 1))
        deps = [c_sum, y_here]
    wide = small_kernel(wide_kernel, both, jnp.float32, COST_W, y_here, *d_here)
    return finish(wide, c_here)


def solution(mesh):
    placed = (
        P(("section", "head"), None, None),
        P(None, "section", "head"),
        P(None, None, "section", None),
        P(None, "section", None),
        P(),
        P("section", "head", None),
    )
    return jax.shard_map(
        on_device,
        mesh=mesh,
        in_specs=placed,
        out_specs=P(("section", "head"), None, None),
        check_vma=False,
    )
```

```python
import functools
import math

import jax
import jax.numpy as jnp
from jax import lax
from jax.experimental import pallas as pl
from jax.experimental.pallas import tpu as pltpu
from jax.sharding import PartitionSpec as P

QH = 32
KVH = 8
HD = 128
GROUP = QH // KVH
KEY_BLOCK = 512
WEIGHT_PARTS = 2
COLUMN_TILE = 1024

neg_large = -1e30
EXPONENT = math.log2(math.e) / math.sqrt(HD)


def scores_of(query_rows, key_rows):
    return lax.dot_general(
        query_rows, key_rows, (((1,), (1,)), ((), ())), preferred_element_type=jnp.float32
    )


def attend(ticks, rows, row_first, my_length, query_of, fresh_ref, cache_ref, heads_ref):
    fresh_count = ticks[-1] + 1
    fresh_rows = fresh_ref.shape[2]
    capacity = cache_ref.shape[1]
    kv_count = fresh_ref.shape[3] // HD
    inner = heads_ref.shape[1] // HD // kv_count
    key_block = min(KEY_BLOCK, capacity)
    tick_rows = inner * rows
    all_rows = len(ticks) * tick_rows
    line = lax.broadcasted_iota(jnp.int32, (all_rows, fresh_rows), 0)
    position = lax.rem(line, rows) + row_first
    causal = lax.broadcasted_iota(jnp.int32, (all_rows, fresh_rows), 1) <= position
    for g in range(kv_count):
        lanes = slice(g * HD, (g + 1) * HD)
        query_rows = jnp.concatenate(
            [
                query_of(index, slice((g * inner + i) * HD, (g * inner + i + 1) * HD))
                for index in range(len(ticks))
                for i in range(inner)
            ],
            axis=0,
        )
        blocks = []
        for earlier in range(fresh_count):
            scores = scores_of(query_rows, fresh_ref[earlier, 0, :, lanes])
            if len(ticks) > 1:
                tick_here = line // tick_rows + ticks[0]
                seen = (tick_here > earlier) | ((tick_here == earlier) & causal)
                scores = jnp.where(seen, scores, neg_large)
            elif earlier == ticks[0]:
                scores = jnp.where(causal, scores, neg_large)
            blocks.append((scores, fresh_ref[earlier, 1, :, lanes]))
        for block in range(capacity // key_block):
            here = slice(block * key_block, (block + 1) * key_block)
            scores = scores_of(query_rows, cache_ref[0, here, lanes])
            column = lax.broadcasted_iota(jnp.int32, (1, key_block), 1)
            scores = scores + jnp.where(column < my_length - block * key_block, 0.0, neg_large)
            blocks.append((scores, cache_ref[1, here, lanes]))
        highest = None
        for scores, _ in blocks:
            for first in range(0, scores.shape[1], HD):
                part = scores[:, first : first + HD]
                highest = part if highest is None else jnp.maximum(highest, part)
        highest = jnp.max(highest, axis=1, keepdims=True)
        total = None
        for scores, values in blocks:
            weights = jnp.exp2((scores - highest) * EXPONENT).astype(jnp.bfloat16)
            wide = jnp.concatenate([values, jnp.ones_like(values)], axis=1)
            added = jnp.dot(weights, wide, preferred_element_type=jnp.float32)
            total = added if total is None else total + added
        mixed = (total[:, :HD] / total[:, HD:]).astype(jnp.bfloat16)
        for index in range(len(ticks)):
            for i in range(inner):
                head = g * inner + i
                first = (index * inner + i) * rows
                heads_ref[
                    index * rows : (index + 1) * rows, head * HD : (head + 1) * HD
                ] = mixed[first : first + rows]


def project(heads_ref, w_ref, outs):
    rows, columns = outs[0].shape
    tile = min(COLUMN_TILE, columns)
    for first in range(0, columns, tile):
        here = slice(first, first + tile)
        product = jnp.dot(heads_ref[...], w_ref[:, here], preferred_element_type=jnp.float32)
        for index, out in enumerate(outs):
            out[:, here] = product[index * rows : (index + 1) * rows].astype(out.dtype)


def project_arriving(heads_ref, w_ref, outs, copies):
    part_columns = w_ref.shape[1] // len(copies)
    for part, copy in enumerate(copies):
        copy.wait()
        here = pl.ds(part * part_columns, part_columns)
        project(heads_ref, w_ref.at[:, here], [out.at[:, here] for out in outs])


def held_copies(new_kv, cache_kv, out_weight, fresh_ref, cache_ref, w_ref, sem):
    kv_width = cache_ref.shape[2]
    heads_here = w_ref.shape[0] // HD
    kv_column = pl.multiple_of(lax.axis_index("head") * heads_here // GROUP * HD, HD)
    lanes = pl.ds(kv_column, kv_width)
    pairs = []
    for tick in range(fresh_ref.shape[0]):
        for part in range(2):
            pairs.append((new_kv.at[tick, part, :, lanes], fresh_ref.at[tick, part]))
    for part in range(2):
        pairs.append((cache_kv.at[part, :, lanes], cache_ref.at[part]))
    part_columns = w_ref.shape[1] // WEIGHT_PARTS
    for part in range(WEIGHT_PARTS):
        here = pl.ds(part * part_columns, part_columns)
        pairs.append((out_weight.at[0, :, here], w_ref.at[:, here]))
    copies = [
        pltpu.make_async_copy(source, target, sem.at[index])
        for index, (source, target) in enumerate(pairs)
    ]
    return copies[:-WEIGHT_PARTS], copies[-WEIGHT_PARTS:]


def first_kernel(
    ticks, rows, choose, active, lengths, queries, new_kv, cache_kv, out_weight, *rest
):
    outs = rest[: len(ticks)]
    fresh_ref, cache_ref, w_ref, length_ref, q_ref, heads_ref, sem = rest[len(ticks) :]
    z = lax.axis_index("head")

    @pl.when(active(z))
    def _():
        row_first = pl.multiple_of(choose(z) * rows, rows)
        copies, w_copies = held_copies(
            new_kv, cache_kv, out_weight, fresh_ref, cache_ref, w_ref, sem
        )
        used = len(copies) + len(w_copies)
        copies.append(pltpu.make_async_copy(lengths, length_ref, sem.at[used]))
        for index, tick in enumerate(ticks):
            copies.append(
                pltpu.make_async_copy(
                    queries.at[tick, pl.ds(row_first, rows), :],
                    q_ref.at[index],
                    sem.at[used + 1 + index],
                )
            )
        for copy in copies[::-1] + w_copies:
            copy.start()
        for copy in copies:
            copy.wait()
        attend(
            ticks,
            rows,
            row_first,
            length_ref[lax.axis_index("section")],
            lambda index, lanes: q_ref[index, :, lanes],
            fresh_ref,
            cache_ref,
            heads_ref,
        )
        project_arriving(heads_ref, w_ref, outs, w_copies)


def later_rows(ticks, rows, choose, lengths, q_ref, fresh_ref, cache_ref, heads_ref):
    row_first = pl.multiple_of(choose(lax.axis_index("head")) * rows, rows)
    attend(
        ticks,
        rows,
        row_first,
        lengths[lax.axis_index("section")],
        lambda index, lanes: q_ref[ticks[index], pl.ds(row_first, rows), lanes],
        fresh_ref,
        cache_ref,
        heads_ref,
    )


def second_kernel(
    ticks,
    rows,
    choose,
    active,
    lengths,
    queries,
    new_kv,
    cache_kv,
    out_weight,
    residual,
    fresh_in,
    cache_in,
    w_in,
    dep,
    *rest,
):
    outs = rest[: len(ticks)]
    q_ref, by_tick_ref, fresh_ref, cache_ref, w_ref, *scratch = rest[len(ticks) :]
    heads_ref, residual_ref, sem, q_sem, residual_sem = scratch
    late = jnp.logical_not(active(lax.axis_index("head")))
    copies, w_copies = held_copies(new_kv, cache_kv, out_weight, fresh_ref, cache_ref, w_ref, sem)
    q_copy = pltpu.make_async_copy(queries, q_ref, q_sem)
    q_copy.start()
    residual_copy = pltpu.make_async_copy(residual, residual_ref, residual_sem)
    residual_copy.start()

    @pl.when(late)
    def _():
        for copy in copies + w_copies:
            copy.start()
        for copy in copies:
            copy.wait()

    q_copy.wait()
    later_rows(ticks, rows, choose, lengths, q_ref, fresh_ref, cache_ref, heads_ref)

    @pl.when(late)
    def _():
        for copy in w_copies:
            copy.wait()

    project(heads_ref, w_ref, outs)
    residual_copy.wait()
    for tick in range(by_tick_ref.shape[0]):
        by_tick_ref[tick] = residual_ref[:, tick, :]


def plus(left, right, out):
    out[...] = (left[...].astype(jnp.float32) + right[...].astype(jnp.float32)).astype(out.dtype)


def rows_kernel(ticks, rows, choose, names, *refs):
    ref = dict(zip(names, refs))
    if "out" in ref:
        outs = [ref["out"].at[index] for index in range(len(ticks))]
    else:
        outs = [ref["out%d" % tick] for tick in ticks]
    later_rows(
        ticks, rows, choose, ref["lengths"], ref["q"], ref["fresh"], ref["cache"], ref["heads"]
    )
    project(ref["heads"], ref["w"], outs)
    if "residual" in ref:
        for index, out in enumerate(outs):
            plus(out, ref["residual"].at[index], out)


def in_vmem(array):
    return pltpu.with_memory_space_constraint(array, pltpu.VMEM)


def in_hbm(array):
    return pltpu.with_memory_space_constraint(array, pltpu.HBM)


WHOLE = pl.BlockSpec(memory_space=pltpu.VMEM)
ANYWHERE = pl.BlockSpec(memory_space=pl.ANY)
PARAMS = pltpu.CompilerParams(vmem_limit_bytes=28 * 2**20)
def cost_of(flops):
    return pl.CostEstimate(flops=flops, bytes_accessed=1000, transcendentals=0)


COST = cost_of(1000)
COST_X = cost_of(1000)
COST_Y = cost_of(4500000000)
COST_SUM = cost_of(1000)
COST_V = cost_of(1000)
COST_CS = cost_of(1000)
COST_W = cost_of(1000)
COST_D = [cost_of(4500000000), cost_of(1000)]


def held_shapes(queries, new_kv, cache_kv, out_weight):
    tick_count, row_count, head_width = queries.shape
    kv_width = max(1, head_width // HD // GROUP) * HD
    kind = queries.dtype
    return [
        pltpu.VMEM((tick_count, 2, row_count, kv_width), kind),
        pltpu.VMEM((2, cache_kv.shape[1], kv_width), kind),
        pltpu.VMEM((head_width, out_weight.shape[2]), kind),
    ]


def first_rows(ticks, rows, choose, active, lengths, *arrays):
    queries, out_weight = arrays[0], arrays[3]
    tick_count, row_count, head_width = queries.shape
    columns = out_weight.shape[2]
    kind = queries.dtype
    out_shape = [pltpu.VMEM((rows, columns), kind)] * len(ticks) + held_shapes(*arrays)
    results = pl.pallas_call(
        functools.partial(first_kernel, ticks, rows, choose, active),
        out_shape=out_shape,
        in_specs=[ANYWHERE] * 5,
        out_specs=[WHOLE] * len(out_shape),
        scratch_shapes=[
            pltpu.SMEM(lengths.shape, lengths.dtype),
            pltpu.VMEM((len(ticks), rows, head_width), kind),
            pltpu.VMEM((len(ticks) * rows, head_width), kind),
            pltpu.SemaphoreType.DMA((3 + 2 * tick_count + WEIGHT_PARTS + len(ticks),)),
        ],
        compiler_params=PARAMS,
        cost_estimate=COST,
    )(*[in_hbm(array) for array in (lengths, *arrays)])
    return results[: len(ticks)], results[len(ticks) :]


def second_rows(ticks, rows, choose, active, lengths, arrays, residual, held, dep):
    queries, out_weight = arrays[0], arrays[3]
    tick_count, row_count, head_width = queries.shape
    kind = queries.dtype
    out_shape = [pltpu.VMEM((rows, out_weight.shape[2]), kind)] * len(ticks)
    out_shape += [
        pltpu.VMEM(queries.shape, kind),
        pltpu.VMEM((tick_count, residual.shape[0], residual.shape[2]), kind),
    ] + held_shapes(*arrays)
    results = pl.pallas_call(
        functools.partial(second_kernel, ticks, rows, choose, active),
        out_shape=out_shape,
        in_specs=[pl.BlockSpec(memory_space=pltpu.SMEM)] + [ANYWHERE] * 5 + [WHOLE] * 3 + [ANYWHERE],
        out_specs=[WHOLE] * len(out_shape),
        scratch_shapes=[
            pltpu.VMEM((len(ticks) * rows, head_width), kind),
            pltpu.VMEM(residual.shape, kind),
            pltpu.SemaphoreType.DMA((2 + 2 * tick_count + WEIGHT_PARTS,)),
            pltpu.SemaphoreType.DMA,
            pltpu.SemaphoreType.DMA,
        ],
        input_output_aliases={6 + index: len(ticks) + 2 + index for index in range(3)},
        compiler_params=PARAMS,
        cost_estimate=COST,
    )(
        lengths,
        *[in_hbm(array) for array in (*arrays, residual)],
        *[in_vmem(array) for array in held],
        dep,
    )
    here = len(ticks)
    return results[:here], results[here + 1], (lengths, results[here], *results[here + 2 :])


def project_rows(ticks, rows, choose, held, cost, deps, residual=None, split=True):
    lengths, queries, fresh, cache, weight = held
    columns = weight.shape[1]
    kind = queries.dtype
    operands = {"q": queries, "fresh": fresh, "cache": cache, "w": weight}
    if residual is not None:
        operands["residual"] = residual
    names = ["lengths"] + list(operands) + ["dep"] * len(deps)
    if split:
        outs = {"out%d" % tick: pltpu.VMEM((rows, columns), kind) for tick in ticks}
    else:
        outs = {"out": pltpu.VMEM((len(ticks), rows, columns), kind)}
    names += list(outs) + ["heads"]
    return pl.pallas_call(
        functools.partial(rows_kernel, ticks, rows, choose, names),
        out_shape=list(outs.values()),
        in_specs=[pl.BlockSpec(memory_space=pltpu.SMEM)]
        + [WHOLE] * len(operands)
        + [ANYWHERE] * len(deps),
        out_specs=[WHOLE] * len(outs),
        scratch_shapes=[pltpu.VMEM((len(ticks) * rows, queries.shape[2]), kind)],
        compiler_params=PARAMS,
        cost_estimate=cost,
    )(lengths, *[in_vmem(array) for array in operands.values()], *deps)


def small_kernel(kernel, shape, kind, cost, *blocks, deps=()):
    return pl.pallas_call(
        kernel,
        out_shape=pltpu.VMEM(shape, kind),
        in_specs=[WHOLE] * len(blocks) + [ANYWHERE] * len(deps),
        out_specs=WHOLE,
        compiler_params=PARAMS,
        cost_estimate=cost,
    )(*blocks, *deps)


def add_kernel(left, right, *rest):
    plus(left, right, rest[-1])


def by_role_kernel(active, count, *refs):
    out = refs[-1]
    plain, left, right = refs[:count], refs[count : 2 * count], refs[2 * count : 3 * count]
    here = active(lax.axis_index("head"))

    @pl.when(here)
    def _():
        for index in range(count):
            plus(left[index], right[index], out.at[index])

    @pl.when(jnp.logical_not(here))
    def _():
        for index in range(count):
            out[index] = plain[index][...]


def inner_kernel(active, tick, plain, left, right, *rest):
    out = rest[-1]
    here = active(lax.axis_index("head"))

    @pl.when(here)
    def _():
        plus(left, right, out)

    @pl.when(jnp.logical_not(here))
    def _():
        out[...] = plain[tick]


def wide_kernel(block, *refs):
    out = refs[-1]
    for tick in range(out.shape[0]):
        out[tick] = block[tick].astype(jnp.float32) + refs[tick][...].astype(jnp.float32)


def finish_kernel(wide, block, out, buf, sem):
    step = 16
    copies = []
    for first in range(0, out.shape[0], step):
        here = pl.ds(first, step)
        for tick in range(out.shape[1]):
            total = wide[tick, here, :] + block[tick, here, :].astype(jnp.float32)
            buf[here, tick, :] = total.astype(out.dtype)
        copies.append(pltpu.make_async_copy(buf.at[here], out.at[here], sem.at[first // step]))
        copies[-1].start()
    for copy in copies:
        copy.wait()


def finish(wide, block):
    tick_count, rows, columns = wide.shape
    shape = (rows, tick_count, columns)
    return pl.pallas_call(
        finish_kernel,
        out_shape=jax.ShapeDtypeStruct(shape, block.dtype),
        in_specs=[WHOLE] * 2,
        out_specs=ANYWHERE,
        scratch_shapes=[
            pltpu.VMEM(shape, block.dtype),
            pltpu.SemaphoreType.DMA((rows // 16,)),
        ],
        compiler_params=PARAMS,
        cost_estimate=COST,
    )(in_vmem(wide), in_vmem(block))


def add(left, right):
    return (left.astype(jnp.float32) + right.astype(jnp.float32)).astype(jnp.bfloat16)


def on_device(residual, queries, new_kv, cache_kv, lengths, out_weight):
    section_count = lax.axis_size("section")
    head_count = lax.axis_size("head")
    tick_count, row_count, head_width = queries.shape
    arrays = (queries, new_kv, cache_kv, out_weight)
    rows = row_count // head_count
    ticks = tuple(range(tick_count))

    def send(block, pairs, distance):
        route = [
            (s * head_count + a, (s + distance) % section_count * head_count + b)
            for s in range(section_count)
            for a, b in pairs
        ]
        return lax.ppermute(block, ("section", "head"), route)

    if head_count != 4 or tick_count != 2:
        partial, _ = first_rows(ticks, row_count, lambda z: 0, lambda z: z >= 0, lengths, *arrays)
        pieces = [
            lax.psum_scatter(block, "head", scatter_dimension=0, tiled=True) for block in partial
        ]
        updated = add(residual, jnp.stack(pieces, axis=1))
        return send(updated, [(i, i) for i in range(head_count)], 1)

    ends = [(0, 1), (3, 2)]
    middle = [(1, 2), (2, 1)]
    outward = [(0, 1), (3, 2), (1, 0), (2, 3)]

    def first(z):
        return jnp.where(z < 2, 3, 0)

    def second(z):
        return jnp.where(z < 2, 2, 1)

    def third(z):
        return jnp.where(z == 0, 1, jnp.where(z == 1, 0, jnp.where(z == 2, 3, 2)))

    def at_end(z):
        return (z == 0) | (z == head_count - 1)

    def in_middle(z):
        return jnp.logical_not(at_end(z))

    def by_role(at_ends, in_the_middle):
        return lambda z: jnp.where(at_end(z), at_ends(z), in_the_middle(z))

    (a0_early,), loaded = first_rows((0,), rows, first, at_end, lengths, *arrays)
    a0_far = send(a0_early, ends, 0)
    (a0, a1), own_residual, held = second_rows(
        ticks, rows, first, at_end, lengths, arrays, residual, loaded, a0_early
    )
    a1_far = send(a1, ends, 0)
    x = project_rows(ticks, rows, by_role(second, third), held, COST_X, [a1])
    x_far = [send(block, ends, 0) for block in x]
    a0_sum = small_kernel(add_kernel, a0.shape, a0.dtype, COST, a0, a0_far, deps=[x[0]])
    a0_mid = send(a0_sum, middle, 0)
    (y,) = project_rows(
        ticks, rows, lambda z: z, held, COST_Y, [a0_sum], own_residual, split=False
    )
    y_here = send(y, [(1, 1), (2, 2)], 1)
    a1_sum = small_kernel(add_kernel, a1.shape, a1.dtype, COST_SUM, a1, a1_far, deps=[y])
    a1_mid = send(a1_sum, middle, 0)
    v = project_rows(
        ticks, rows, by_role(third, second), held, COST_V, [a1_sum, a0_mid, x_far[0]]
    )
    both = (tick_count,) + a0.shape
    c_sum = small_kernel(
        functools.partial(by_role_kernel, in_middle, tick_count),
        both,
        a0.dtype,
        COST_CS,
        *v,
        *x,
        a0_mid,
        a1_mid,
    )
    c_here = send(c_sum, outward, 1)
    d_here = []
    deps = [c_sum]
    for tick in ticks:
        d_sum = small_kernel(
            functools.partial(inner_kernel, in_middle, tick),
            a0.shape,
            a0.dtype,
            COST_D[tick],
            y,
            v[tick],
            x_far[tick],
            deps=deps,
        )
        d_here.append(send(d_sum, middle + [(0, 0), (3, 3)], 1))
        deps = [c_sum, y_here]
    wide = small_kernel(wide_kernel, both, jnp.float32, COST_W, y_here, *d_here)
    return finish(wide, c_here)


def solution(mesh):
    placed = (
        P(("section", "head"), None, None),
        P(None, "section", "head"),
        P(None, None, "section", None),
        P(None, "section", None),
        P(),
        P("section", "head", None),
    )
    return jax.shard_map(
        on_device,
        mesh=mesh,
        in_specs=placed,
        out_specs=P(("section", "head"), None, None),
        check_vma=False,
    )
```

```python
import functools
import math

import jax
import jax.numpy as jnp
from jax import lax
from jax.experimental import pallas as pl
from jax.experimental.pallas import tpu as pltpu
from jax.sharding import PartitionSpec as P

QH = 32
KVH = 8
HD = 128
GROUP = QH // KVH
KEY_BLOCK = 512
WEIGHT_PARTS = 2
COLUMN_TILE = 1024

neg_large = -1e30
EXPONENT = math.log2(math.e) / math.sqrt(HD)


def scores_of(query_rows, key_rows):
    return lax.dot_general(
        query_rows, key_rows, (((1,), (1,)), ((), ())), preferred_element_type=jnp.float32
    )


def attend(ticks, rows, row_first, my_length, query_of, fresh_ref, cache_ref, heads_ref):
    fresh_count = ticks[-1] + 1
    fresh_rows = fresh_ref.shape[2]
    capacity = cache_ref.shape[1]
    kv_count = fresh_ref.shape[3] // HD
    inner = heads_ref.shape[1] // HD // kv_count
    key_block = min(KEY_BLOCK, capacity)
    tick_rows = inner * rows
    all_rows = len(ticks) * tick_rows
    line = lax.broadcasted_iota(jnp.int32, (all_rows, fresh_rows), 0)
    position = lax.rem(line, rows) + row_first
    causal = lax.broadcasted_iota(jnp.int32, (all_rows, fresh_rows), 1) <= position
    for g in range(kv_count):
        lanes = slice(g * HD, (g + 1) * HD)
        query_rows = jnp.concatenate(
            [
                query_of(index, slice((g * inner + i) * HD, (g * inner + i + 1) * HD))
                for index in range(len(ticks))
                for i in range(inner)
            ],
            axis=0,
        )
        blocks = []
        for earlier in range(fresh_count):
            scores = scores_of(query_rows, fresh_ref[earlier, 0, :, lanes])
            if len(ticks) > 1:
                tick_here = line // tick_rows + ticks[0]
                seen = (tick_here > earlier) | ((tick_here == earlier) & causal)
                scores = jnp.where(seen, scores, neg_large)
            elif earlier == ticks[0]:
                scores = jnp.where(causal, scores, neg_large)
            blocks.append((scores, fresh_ref[earlier, 1, :, lanes]))
        for block in range(capacity // key_block):
            here = slice(block * key_block, (block + 1) * key_block)
            scores = scores_of(query_rows, cache_ref[0, here, lanes])
            column = lax.broadcasted_iota(jnp.int32, (1, key_block), 1)
            scores = scores + jnp.where(column < my_length - block * key_block, 0.0, neg_large)
            blocks.append((scores, cache_ref[1, here, lanes]))
        highest = None
        for scores, _ in blocks:
            for first in range(0, scores.shape[1], HD):
                part = scores[:, first : first + HD]
                highest = part if highest is None else jnp.maximum(highest, part)
        highest = jnp.max(highest, axis=1, keepdims=True)
        total = None
        for scores, values in blocks:
            weights = jnp.exp2((scores - highest) * EXPONENT).astype(jnp.bfloat16)
            wide = jnp.concatenate([values, jnp.ones_like(values)], axis=1)
            added = jnp.dot(weights, wide, preferred_element_type=jnp.float32)
            total = added if total is None else total + added
        mixed = (total[:, :HD] / total[:, HD:]).astype(jnp.bfloat16)
        for index in range(len(ticks)):
            for i in range(inner):
                head = g * inner + i
                first = (index * inner + i) * rows
                heads_ref[
                    index * rows : (index + 1) * rows, head * HD : (head + 1) * HD
                ] = mixed[first : first + rows]


def project(heads_ref, w_ref, outs):
    rows, columns = outs[0].shape
    tile = min(COLUMN_TILE, columns)
    for first in range(0, columns, tile):
        here = slice(first, first + tile)
        product = jnp.dot(heads_ref[...], w_ref[:, here], preferred_element_type=jnp.float32)
        for index, out in enumerate(outs):
            out[:, here] = product[index * rows : (index + 1) * rows].astype(out.dtype)


def weight_parts(columns):
    most = columns * 3 // 4
    return [pl.ds(0, most), pl.ds(most, columns - most)]


def project_arriving(heads_ref, w_ref, outs, copies):
    for here, copy in zip(weight_parts(w_ref.shape[1]), copies):
        copy.wait()
        project(heads_ref, w_ref.at[:, here], [out.at[:, here] for out in outs])


def held_copies(new_kv, cache_kv, out_weight, fresh_ref, cache_ref, w_ref, sem):
    kv_width = cache_ref.shape[2]
    heads_here = w_ref.shape[0] // HD
    kv_column = pl.multiple_of(lax.axis_index("head") * heads_here // GROUP * HD, HD)
    lanes = pl.ds(kv_column, kv_width)
    pairs = []
    for tick in range(fresh_ref.shape[0]):
        for part in range(2):
            pairs.append((new_kv.at[tick, part, :, lanes], fresh_ref.at[tick, part]))
    for part in range(2):
        pairs.append((cache_kv.at[part, :, lanes], cache_ref.at[part]))
    for here in weight_parts(w_ref.shape[1]):
        pairs.append((out_weight.at[0, :, here], w_ref.at[:, here]))
    copies = [
        pltpu.make_async_copy(source, target, sem.at[index])
        for index, (source, target) in enumerate(pairs)
    ]
    return copies[:-WEIGHT_PARTS], copies[-WEIGHT_PARTS:]


def first_kernel(
    ticks, rows, choose, active, lengths, queries, new_kv, cache_kv, out_weight, *rest
):
    outs = rest[: len(ticks)]
    fresh_ref, cache_ref, w_ref, length_ref, q_ref, heads_ref, sem = rest[len(ticks) :]
    z = lax.axis_index("head")

    @pl.when(active(z))
    def _():
        row_first = pl.multiple_of(choose(z) * rows, rows)
        copies, w_copies = held_copies(
            new_kv, cache_kv, out_weight, fresh_ref, cache_ref, w_ref, sem
        )
        used = len(copies) + len(w_copies)
        copies.append(pltpu.make_async_copy(lengths, length_ref, sem.at[used]))
        for index, tick in enumerate(ticks):
            copies.append(
                pltpu.make_async_copy(
                    queries.at[tick, pl.ds(row_first, rows), :],
                    q_ref.at[index],
                    sem.at[used + 1 + index],
                )
            )
        for copy in copies[::-1] + w_copies:
            copy.start()
        for copy in copies:
            copy.wait()
        attend(
            ticks,
            rows,
            row_first,
            length_ref[lax.axis_index("section")],
            lambda index, lanes: q_ref[index, :, lanes],
            fresh_ref,
            cache_ref,
            heads_ref,
        )
        project_arriving(heads_ref, w_ref, outs, w_copies)


def later_rows(ticks, rows, choose, lengths, q_ref, fresh_ref, cache_ref, heads_ref):
    row_first = pl.multiple_of(choose(lax.axis_index("head")) * rows, rows)
    attend(
        ticks,
        rows,
        row_first,
        lengths[lax.axis_index("section")],
        lambda index, lanes: q_ref[ticks[index], pl.ds(row_first, rows), lanes],
        fresh_ref,
        cache_ref,
        heads_ref,
    )


def second_kernel(
    ticks,
    rows,
    choose,
    active,
    lengths,
    queries,
    new_kv,
    cache_kv,
    out_weight,
    residual,
    fresh_in,
    cache_in,
    w_in,
    dep,
    *rest,
):
    outs = rest[: len(ticks)]
    q_ref, by_tick_ref, fresh_ref, cache_ref, w_ref, *scratch = rest[len(ticks) :]
    heads_ref, residual_ref, sem, q_sem, residual_sem = scratch
    late = jnp.logical_not(active(lax.axis_index("head")))
    copies, w_copies = held_copies(new_kv, cache_kv, out_weight, fresh_ref, cache_ref, w_ref, sem)
    q_copy = pltpu.make_async_copy(queries, q_ref, q_sem)
    q_copy.start()
    residual_copy = pltpu.make_async_copy(residual, residual_ref, residual_sem)
    residual_copy.start()

    @pl.when(late)
    def _():
        for copy in copies + w_copies:
            copy.start()
        for copy in copies:
            copy.wait()

    q_copy.wait()
    later_rows(ticks, rows, choose, lengths, q_ref, fresh_ref, cache_ref, heads_ref)

    @pl.when(late)
    def _():
        for copy in w_copies:
            copy.wait()

    project(heads_ref, w_ref, outs)
    residual_copy.wait()
    for tick in range(by_tick_ref.shape[0]):
        by_tick_ref[tick] = residual_ref[:, tick, :]


def plus(left, right, out):
    out[...] = (left[...].astype(jnp.float32) + right[...].astype(jnp.float32)).astype(out.dtype)


def rows_kernel(ticks, rows, choose, names, *refs):
    ref = dict(zip(names, refs))
    if "out" in ref:
        outs = [ref["out"].at[index] for index in range(len(ticks))]
    else:
        outs = [ref["out%d" % tick] for tick in ticks]
    later_rows(
        ticks, rows, choose, ref["lengths"], ref["q"], ref["fresh"], ref["cache"], ref["heads"]
    )
    project(ref["heads"], ref["w"], outs)
    if "residual" in ref:
        for index, out in enumerate(outs):
            plus(out, ref["residual"].at[index], out)


def in_vmem(array):
    return pltpu.with_memory_space_constraint(array, pltpu.VMEM)


def in_hbm(array):
    return pltpu.with_memory_space_constraint(array, pltpu.HBM)


WHOLE = pl.BlockSpec(memory_space=pltpu.VMEM)
ANYWHERE = pl.BlockSpec(memory_space=pl.ANY)
PARAMS = pltpu.CompilerParams(vmem_limit_bytes=28 * 2**20)
def cost_of(flops):
    return pl.CostEstimate(flops=flops, bytes_accessed=1000, transcendentals=0)


COST = cost_of(1000)
COST_X = cost_of(1000)
COST_Y = cost_of(4500000000)
COST_SUM = cost_of(1000)
COST_V = cost_of(1000)
COST_CS = cost_of(1000)
COST_W = cost_of(1000)
COST_D = [cost_of(4500000000), cost_of(1000)]


def held_shapes(queries, new_kv, cache_kv, out_weight):
    tick_count, row_count, head_width = queries.shape
    kv_width = max(1, head_width // HD // GROUP) * HD
    kind = queries.dtype
    return [
        pltpu.VMEM((tick_count, 2, row_count, kv_width), kind),
        pltpu.VMEM((2, cache_kv.shape[1], kv_width), kind),
        pltpu.VMEM((head_width, out_weight.shape[2]), kind),
    ]


def first_rows(ticks, rows, choose, active, lengths, *arrays):
    queries, out_weight = arrays[0], arrays[3]
    tick_count, row_count, head_width = queries.shape
    columns = out_weight.shape[2]
    kind = queries.dtype
    out_shape = [pltpu.VMEM((rows, columns), kind)] * len(ticks) + held_shapes(*arrays)
    results = pl.pallas_call(
        functools.partial(first_kernel, ticks, rows, choose, active),
        out_shape=out_shape,
        in_specs=[ANYWHERE] * 5,
        out_specs=[WHOLE] * len(out_shape),
        scratch_shapes=[
            pltpu.SMEM(lengths.shape, lengths.dtype),
            pltpu.VMEM((len(ticks), rows, head_width), kind),
            pltpu.VMEM((len(ticks) * rows, head_width), kind),
            pltpu.SemaphoreType.DMA((3 + 2 * tick_count + WEIGHT_PARTS + len(ticks),)),
        ],
        compiler_params=PARAMS,
        cost_estimate=COST,
    )(*[in_hbm(array) for array in (lengths, *arrays)])
    return results[: len(ticks)], results[len(ticks) :]


def second_rows(ticks, rows, choose, active, lengths, arrays, residual, held, dep):
    queries, out_weight = arrays[0], arrays[3]
    tick_count, row_count, head_width = queries.shape
    kind = queries.dtype
    out_shape = [pltpu.VMEM((rows, out_weight.shape[2]), kind)] * len(ticks)
    out_shape += [
        pltpu.VMEM(queries.shape, kind),
        pltpu.VMEM((tick_count, residual.shape[0], residual.shape[2]), kind),
    ] + held_shapes(*arrays)
    results = pl.pallas_call(
        functools.partial(second_kernel, ticks, rows, choose, active),
        out_shape=out_shape,
        in_specs=[pl.BlockSpec(memory_space=pltpu.SMEM)] + [ANYWHERE] * 5 + [WHOLE] * 3 + [ANYWHERE],
        out_specs=[WHOLE] * len(out_shape),
        scratch_shapes=[
            pltpu.VMEM((len(ticks) * rows, head_width), kind),
            pltpu.VMEM(residual.shape, kind),
            pltpu.SemaphoreType.DMA((2 + 2 * tick_count + WEIGHT_PARTS,)),
            pltpu.SemaphoreType.DMA,
            pltpu.SemaphoreType.DMA,
        ],
        input_output_aliases={6 + index: len(ticks) + 2 + index for index in range(3)},
        compiler_params=PARAMS,
        cost_estimate=COST,
    )(
        lengths,
        *[in_hbm(array) for array in (*arrays, residual)],
        *[in_vmem(array) for array in held],
        dep,
    )
    here = len(ticks)
    return results[:here], results[here + 1], (lengths, results[here], *results[here + 2 :])


def project_rows(ticks, rows, choose, held, cost, deps, residual=None, split=True):
    lengths, queries, fresh, cache, weight = held
    columns = weight.shape[1]
    kind = queries.dtype
    operands = {"q": queries, "fresh": fresh, "cache": cache, "w": weight}
    if residual is not None:
        operands["residual"] = residual
    names = ["lengths"] + list(operands) + ["dep"] * len(deps)
    if split:
        outs = {"out%d" % tick: pltpu.VMEM((rows, columns), kind) for tick in ticks}
    else:
        outs = {"out": pltpu.VMEM((len(ticks), rows, columns), kind)}
    names += list(outs) + ["heads"]
    return pl.pallas_call(
        functools.partial(rows_kernel, ticks, rows, choose, names),
        out_shape=list(outs.values()),
        in_specs=[pl.BlockSpec(memory_space=pltpu.SMEM)]
        + [WHOLE] * len(operands)
        + [ANYWHERE] * len(deps),
        out_specs=[WHOLE] * len(outs),
        scratch_shapes=[pltpu.VMEM((len(ticks) * rows, queries.shape[2]), kind)],
        compiler_params=PARAMS,
        cost_estimate=cost,
    )(lengths, *[in_vmem(array) for array in operands.values()], *deps)


def small_kernel(kernel, shape, kind, cost, *blocks, deps=()):
    return pl.pallas_call(
        kernel,
        out_shape=pltpu.VMEM(shape, kind),
        in_specs=[WHOLE] * len(blocks) + [ANYWHERE] * len(deps),
        out_specs=WHOLE,
        compiler_params=PARAMS,
        cost_estimate=cost,
    )(*blocks, *deps)


def add_kernel(left, right, *rest):
    plus(left, right, rest[-1])


def by_role_kernel(active, count, *refs):
    out = refs[-1]
    plain, left, right = refs[:count], refs[count : 2 * count], refs[2 * count : 3 * count]
    here = active(lax.axis_index("head"))

    @pl.when(here)
    def _():
        for index in range(count):
            plus(left[index], right[index], out.at[index])

    @pl.when(jnp.logical_not(here))
    def _():
        for index in range(count):
            out[index] = plain[index][...]


def inner_kernel(active, tick, plain, left, right, *rest):
    out = rest[-1]
    here = active(lax.axis_index("head"))

    @pl.when(here)
    def _():
        plus(left, right, out)

    @pl.when(jnp.logical_not(here))
    def _():
        out[...] = plain[tick]


def wide_kernel(block, *refs):
    out = refs[-1]
    for tick in range(out.shape[0]):
        out[tick] = block[tick].astype(jnp.float32) + refs[tick][...].astype(jnp.float32)


def finish_kernel(wide, block, out, buf, sem):
    step = 16
    copies = []
    for first in range(0, out.shape[0], step):
        here = pl.ds(first, step)
        for tick in range(out.shape[1]):
            total = wide[tick, here, :] + block[tick, here, :].astype(jnp.float32)
            buf[here, tick, :] = total.astype(out.dtype)
        copies.append(pltpu.make_async_copy(buf.at[here], out.at[here], sem.at[first // step]))
        copies[-1].start()
    for copy in copies:
        copy.wait()


def finish(wide, block):
    tick_count, rows, columns = wide.shape
    shape = (rows, tick_count, columns)
    return pl.pallas_call(
        finish_kernel,
        out_shape=jax.ShapeDtypeStruct(shape, block.dtype),
        in_specs=[WHOLE] * 2,
        out_specs=ANYWHERE,
        scratch_shapes=[
            pltpu.VMEM(shape, block.dtype),
            pltpu.SemaphoreType.DMA((rows // 16,)),
        ],
        compiler_params=PARAMS,
        cost_estimate=COST,
    )(in_vmem(wide), in_vmem(block))


def add(left, right):
    return (left.astype(jnp.float32) + right.astype(jnp.float32)).astype(jnp.bfloat16)


def on_device(residual, queries, new_kv, cache_kv, lengths, out_weight):
    section_count = lax.axis_size("section")
    head_count = lax.axis_size("head")
    tick_count, row_count, head_width = queries.shape
    arrays = (queries, new_kv, cache_kv, out_weight)
    rows = row_count // head_count
    ticks = tuple(range(tick_count))

    def send(block, pairs, distance):
        route = [
            (s * head_count + a, (s + distance) % section_count * head_count + b)
            for s in range(section_count)
            for a, b in pairs
        ]
        return lax.ppermute(block, ("section", "head"), route)

    if head_count != 4 or tick_count != 2:
        partial, _ = first_rows(ticks, row_count, lambda z: 0, lambda z: z >= 0, lengths, *arrays)
        pieces = [
            lax.psum_scatter(block, "head", scatter_dimension=0, tiled=True) for block in partial
        ]
        updated = add(residual, jnp.stack(pieces, axis=1))
        return send(updated, [(i, i) for i in range(head_count)], 1)

    ends = [(0, 1), (3, 2)]
    middle = [(1, 2), (2, 1)]
    outward = [(0, 1), (3, 2), (1, 0), (2, 3)]

    def first(z):
        return jnp.where(z < 2, 3, 0)

    def second(z):
        return jnp.where(z < 2, 2, 1)

    def third(z):
        return jnp.where(z == 0, 1, jnp.where(z == 1, 0, jnp.where(z == 2, 3, 2)))

    def at_end(z):
        return (z == 0) | (z == head_count - 1)

    def in_middle(z):
        return jnp.logical_not(at_end(z))

    def by_role(at_ends, in_the_middle):
        return lambda z: jnp.where(at_end(z), at_ends(z), in_the_middle(z))

    (a0_early,), loaded = first_rows((0,), rows, first, at_end, lengths, *arrays)
    a0_far = send(a0_early, ends, 0)
    (a0, a1), own_residual, held = second_rows(
        ticks, rows, first, at_end, lengths, arrays, residual, loaded, a0_early
    )
    a1_far = send(a1, ends, 0)
    x = project_rows(ticks, rows, by_role(second, third), held, COST_X, [a1])
    x_far = [send(block, ends, 0) for block in x]
    a0_sum = small_kernel(add_kernel, a0.shape, a0.dtype, COST, a0, a0_far, deps=[x[0]])
    a0_mid = send(a0_sum, middle, 0)
    (y,) = project_rows(
        ticks, rows, lambda z: z, held, COST_Y, [a0_sum], own_residual, split=False
    )
    y_here = send(y, [(1, 1), (2, 2)], 1)
    a1_sum = small_kernel(add_kernel, a1.shape, a1.dtype, COST_SUM, a1, a1_far, deps=[y])
    a1_mid = send(a1_sum, middle, 0)
    v = project_rows(
        ticks, rows, by_role(third, second), held, COST_V, [a1_sum, a0_mid, x_far[0]]
    )
    both = (tick_count,) + a0.shape
    c_sum = small_kernel(
        functools.partial(by_role_kernel, in_middle, tick_count),
        both,
        a0.dtype,
        COST_CS,
        *v,
        *x,
        a0_mid,
        a1_mid,
    )
    c_here = send(c_sum, outward, 1)
    d_here = []
    deps = [c_sum]
    for tick in ticks:
        d_sum = small_kernel(
            functools.partial(inner_kernel, in_middle, tick),
            a0.shape,
            a0.dtype,
            COST_D[tick],
            y,
            v[tick],
            x_far[tick],
            deps=deps,
        )
        d_here.append(send(d_sum, middle + [(0, 0), (3, 3)], 1))
        deps = [c_sum, y_here]
    wide = small_kernel(wide_kernel, both, jnp.float32, COST_W, y_here, *d_here)
    return finish(wide, c_here)


def solution(mesh):
    placed = (
        P(("section", "head"), None, None),
        P(None, "section", "head"),
        P(None, None, "section", None),
        P(None, "section", None),
        P(),
        P("section", "head", None),
    )
    return jax.shard_map(
        on_device,
        mesh=mesh,
        in_specs=placed,
        out_specs=P(("section", "head"), None, None),
        check_vma=False,
    )
```
